128 devices in a mesh: dp: 8 (over y, z_hi), seq: 16 (over z_lo, x, core).
Axes of the slice: x: 4, y: 4, z: 4 (z_hi: 2, z_lo: 2; z = z_hi * 2 + z_lo), core: 2. Of those that a mesh axis runs over, the one named last changes fastest.
Arguments:
- bases: int32 [4194304], P(('dp', 'seq')), parts along dimension 0, may hold values from 0 to 3
- stem_weight: bfloat16 [20, 768], replicated, may hold values from -2.5 to 2.5
- conv_weight: bfloat16 [5, 768, 1536], replicated, may hold values from -0.09375 to 0.09375
- row_proj: bfloat16 [1536, 128], replicated, may hold values from -0.15625 to 0.15625
- col_proj: bfloat16 [1536, 128], replicated, may hold values from -0.15625 to 0.15625
- pair_weight: bfloat16 [3, 3, 128, 128], replicated, may hold values from -0.1875 to 0.1875
- out_weight: bfloat16 [128], replicated, may hold values from -0.5 to 0.5
- targets: int32 [2048, 256], P(('dp', 'seq')), parts along dimension 0, may hold values from 0 to 15
Outputs:
- predicted: float32 [2048, 256], P(('dp', 'seq')), parts along dimension 0
- trunk_grad: float32 [2048, 1536], P(('dp', 'seq')), parts along dimension 0
The draws below stay inside these ranges and needn't reach their ends.
There are 8 independent parts, one for each index of `dp`. The reference program is written for one: setup_inputs(seed, part) draws one part's arguments, and reference() takes and returns one part's arrays. A program takes and returns all parts, laid end to end along the dimension named above; an argument that names none is the same for every part. Nothing has to cross between parts.
All inputs are finite; a program needn't handle non-finite values.
Results may differ from the reference program's by a relative error of at most 0.015.
The reference program's roundings to bfloat16 on the way count: a program that leaves them out, or rounds other values in their place, can miss the bound.
Values may be sent and summed in bfloat16 or wider, within the bound.
A program may use at most 128 MiB of HBM per device.

```python
import math
import jax
import jax.numpy as jnp
from jax import lax

STEM_CH = 768
TRUNK_CH = 1536
PAIR_CH = 128
STEM_POOL = 128
TRUNK_POOL = 16
PAIR_DILATION = 8
NBINS = 16
BASES = 524288
BINS = 256


def set_ends(entries, own_key, low, top_value):
    longest = entries.shape.index(max(entries.shape))
    spots = []
    for shift in (0, 1):
        where = [jax.random.randint(jax.random.fold_in(own_key, axis), (), 0, length) for axis, length in enumerate(entries.shape)]
        where[longest] = (where[longest] + shift) % entries.shape[longest]
        spots.append(tuple(where))
    return entries.at[spots[0]].set(low).at[spots[1]].set(top_value)


def scatter_about(key, dims, spread, limit, kind=jnp.bfloat16):
    return jnp.clip(spread * jax.random.normal(key, dims, jnp.float32), -limit, limit).astype(kind)


def setup_inputs(seed: int = 0, part: int = 0) -> dict:
    key_list = jax.random.split(jax.random.key(seed), 9)
    own_keys = jax.random.split(jax.random.fold_in(key_list[8], part), 9)
    bases = set_ends(jax.random.randint(own_keys[0], (BASES,), 0, 4), jax.random.fold_in(own_keys[0], 1), 0, 3).astype(jnp.int32)
    stem_weight = scatter_about(key_list[1], (20, STEM_CH), 5 ** -0.5, 2.5)
    conv_weight = scatter_about(key_list[2], (5, STEM_CH, TRUNK_CH), (5 * STEM_CH) ** -0.5, 0.09375)
    row_proj = scatter_about(key_list[3], (TRUNK_CH, PAIR_CH), TRUNK_CH ** -0.5, 0.15625)
    col_proj = scatter_about(key_list[4], (TRUNK_CH, PAIR_CH), TRUNK_CH ** -0.5, 0.15625)
    pair_weight = scatter_about(key_list[5], (3, 3, PAIR_CH, PAIR_CH), (9 * PAIR_CH) ** -0.5, 0.1875)
    out_weight = scatter_about(key_list[6], (PAIR_CH,), PAIR_CH ** -0.5, 0.5)
    targets = set_ends(jax.random.randint(own_keys[7], (BINS, BINS), 0, NBINS), jax.random.fold_in(own_keys[7], 1), 0, NBINS - 1).astype(jnp.int32)
    return {"bases": bases, "stem_weight": stem_weight, "conv_weight": conv_weight, "row_proj": row_proj, "col_proj": col_proj, "pair_weight": pair_weight, "out_weight": out_weight, "targets": targets}


def gelu_slope(values):
    return jax.grad(lambda inner: jnp.sum(jax.nn.gelu(inner)))(values)

def stem_block(padded, first_row, stem_weight, block_len):
    window = lax.dynamic_slice_in_dim(padded, first_row, block_len + 4)
    base_codes = jnp.arange(1, 5, dtype=jnp.int32)
    columns = [window[offset:offset + block_len, None] == base_codes[None, :] for offset in range(5)]
    onehot = jnp.concatenate(columns, axis=1).astype(jnp.bfloat16)
    activated = jax.nn.gelu(jnp.dot(onehot, stem_weight, preferred_element_type=jnp.float32))
    shaped = activated.reshape(block_len // STEM_POOL, STEM_POOL, activated.shape[1])
    return lax.optimization_barrier(jnp.max(shaped, axis=1)).astype(jnp.bfloat16)

def trunk_conv(extended, conv_weight, row_count):
    total_sum = jnp.zeros((row_count, conv_weight.shape[2]), jnp.float32)
    for offset in range(5):
        total_sum = total_sum + jnp.dot(extended[offset:offset + row_count], conv_weight[offset], preferred_element_type=jnp.float32)
    activated = jax.nn.gelu(total_sum)
    shaped = activated.reshape(row_count // TRUNK_POOL, TRUNK_POOL, activated.shape[1])
    return lax.optimization_barrier(jnp.max(shaped, axis=1))

def pair_taps(padded, weight, row_count, col_count, reverse):
    channels = weight.shape[3]
    total_sum = jnp.zeros((row_count * col_count, channels), jnp.float32)
    for kernel_row in range(3):
        for kernel_column in range(3):
            if reverse:
                row_begin = (2 - kernel_row) * PAIR_DILATION
                column_begin = (2 - kernel_column) * PAIR_DILATION
                matrix = weight[kernel_row, kernel_column].T
            else:
                row_begin = kernel_row * PAIR_DILATION
                column_begin = kernel_column * PAIR_DILATION
                matrix = weight[kernel_row, kernel_column]
            window = padded[row_begin:row_begin + row_count, column_begin:column_begin + col_count]
            window = window.reshape(row_count * col_count, channels)
            total_sum = total_sum + jnp.dot(window, matrix, preferred_element_type=jnp.float32)
    return total_sum.reshape(row_count, col_count, channels)

def reference(bases, stem_weight, conv_weight, row_proj, col_proj, pair_weight, out_weight, targets):
    block_len = 4096
    padded = jnp.pad(bases + 1, 2)
    starts = (jnp.arange(BASES // block_len) * block_len).astype(jnp.int32)
    pooled1 = lax.map(lambda first_row: stem_block(padded, first_row, stem_weight, block_len), starts)
    pooled1 = pooled1.reshape(BASES // STEM_POOL, STEM_CH)
    extended = jnp.pad(pooled1, ((2, 2), (0, 0)))
    pooled2 = trunk_conv(extended, conv_weight, BASES // STEM_POOL)
    channel_mean = lax.optimization_barrier(jnp.sum(pooled2, axis=0)) / BINS
    channel_var = lax.optimization_barrier(jnp.sum(pooled2 * pooled2, axis=0)) / BINS - channel_mean * channel_mean
    normed = ((pooled2 - channel_mean) * lax.rsqrt(channel_var + 1e-05)).astype(jnp.bfloat16)
    rows_emb = jnp.dot(normed, row_proj, preferred_element_type=jnp.float32).astype(jnp.bfloat16)
    cols_emb = jnp.dot(normed, col_proj, preferred_element_type=jnp.float32).astype(jnp.bfloat16)
    summed = rows_emb.astype(jnp.float32)[:, None, :] + cols_emb.astype(jnp.float32)[None, :, :]
    hidden_state = jax.nn.gelu(summed).astype(jnp.bfloat16)
    hidden_padded = jnp.pad(hidden_state, ((PAIR_DILATION, PAIR_DILATION), (PAIR_DILATION, PAIR_DILATION), (0, 0)))
    conv_out = pair_taps(hidden_padded, pair_weight, BINS, BINS, False)
    out_scale = out_weight.astype(jnp.float32)
    predicted = lax.optimization_barrier(jnp.sum((hidden_state.astype(jnp.float32) + jax.nn.gelu(conv_out)) * out_scale, axis=-1))
    target_value = (targets.astype(jnp.float32) - (NBINS - 1) / 2.0) / (NBINS / 4.0)
    pred_grad = (predicted - target_value) / math.sqrt(BINS)
    direct = pred_grad[:, :, None] * out_scale
    filter_gradient = (direct * gelu_slope(conv_out)).astype(jnp.bfloat16)
    gradient_padded = jnp.pad(filter_gradient, ((PAIR_DILATION, PAIR_DILATION), (PAIR_DILATION, PAIR_DILATION), (0, 0)))
    hidden_grad = direct + pair_taps(gradient_padded, pair_weight, BINS, BINS, True)
    sum_grad = hidden_grad * gelu_slope(summed)
    row_grad = lax.optimization_barrier(jnp.sum(sum_grad, axis=1))
    col_grad = lax.optimization_barrier(jnp.sum(sum_grad, axis=0))
    row_term = jnp.dot(row_grad, row_proj.astype(jnp.float32).T, precision=lax.Precision.HIGHEST, preferred_element_type=jnp.float32)
    col_term = jnp.dot(col_grad, col_proj.astype(jnp.float32).T, precision=lax.Precision.HIGHEST, preferred_element_type=jnp.float32)
    return (predicted, row_term + col_term)
```

```python
import functools
import math

import jax
import jax.numpy as jnp
from jax import lax
from jax.experimental import pallas as pl
from jax.experimental.pallas import tpu as pltpu
from jax.sharding import PartitionSpec as P

MESH = pl.DeviceIdType.MESH
F32 = jnp.float32
BF16 = jnp.bfloat16

N_SEQ = 16
STEM_CH = 768
TRUNK_CH = 1536
CH = 128
POOL = 128
ROWS = 256
BINS = 256
LOCAL = 16
GROUP = 24
TILES = TRUNK_CH // 256
C0 = math.sqrt(2.0 / math.pi)


def gelu(x):
    half = 0.5 * x
    return half + half * jnp.tanh(x * (C0 + (C0 * 0.044715) * (x * x)))


def gelu_and_slope(x):
    square = x * x
    t = jnp.tanh(x * (C0 + (C0 * 0.044715) * square))
    half = 0.5 * x
    slope = 0.5 + 0.5 * t + half * (1.0 - t * t) * (C0 + (3.0 * C0 * 0.044715) * square)
    return half + half * t, slope


def fused(
    bases_ref,
    stem_ref,
    conv_ref,
    row_proj_ref,
    col_proj_ref,
    pair_ref,
    out_w_ref,
    targets_ref,
    pred_ref,
    grad_ref,
    halo,
    ext,
    codes,
    stem_w,
    pooled1,
    lhs,
    conv_w,
    pooled2,
    stat_out,
    stat_in,
    emb_out,
    emb_in,
    tgt_out,
    tgt_in,
    tgt_rows,
    tgt_t,
    fwd_w,
    bwd_w,
    rows_scr,
    hid,
    slope_scr,
    direct_scr,
    cgrad,
    pred_t,
    pred_out_s,
    pred_in,
    rowsum,
    part_out,
    part_in,
    conv_sems,
    halo_send,
    halo_recv,
    send_sems,
    recv_sems,
):
    me = lax.axis_index("seq")
    rho = me // 2
    half = me % 2
    first = me == 0
    last = me == N_SEQ - 1

    for q in range(TILES):
        pltpu.make_async_copy(
            conv_ref.at[:, pl.ds(256 * q, 256)], conv_w.at[q], conv_sems.at[q]
        ).start()

    barrier = pltpu.get_barrier_semaphore()

    def greet(k, carry):
        peer = lax.rem(me + k, N_SEQ)
        pl.semaphore_signal(barrier, inc=1, device_id={"seq": peer}, device_id_type=MESH)
        return carry

    lax.fori_loop(1, N_SEQ, greet, 0)

    ext[...] = jnp.zeros_like(ext)
    ext[8 : 8 + ROWS, :] = bases_ref[...] + 1
    for r in range(8):
        tgt_out[r, 0:1, :] = targets_ref[r : r + 1, :]
        tgt_out[r, 1:2, :] = targets_ref[r + 8 : r + 9, :]
    stem_w[...] = jnp.zeros_like(stem_w)
    stem_w[0:20, :] = stem_ref[...].astype(F32)

    pl.semaphore_wait(barrier, N_SEQ - 1)

    def send_all(index, source_of, landing):
        def one(k, carry):
            peer = lax.rem(me + k, N_SEQ)
            pltpu.make_async_remote_copy(
                src_ref=source_of(peer),
                dst_ref=landing.at[me],
                send_sem=send_sems.at[index],
                recv_sem=recv_sems.at[index],
                device_id={"seq": peer},
                device_id_type=MESH,
            ).start()
            return carry

        lax.fori_loop(1, N_SEQ, one, 0)

    def wait_recv(index, landing):
        blocks = landing.at[pl.ds(0, N_SEQ - 1)]
        pltpu.make_async_copy(blocks, blocks, recv_sems.at[index]).wait()

    def wait_send(index, landing):
        blocks = landing.at[pl.ds(0, N_SEQ - 1)]
        pltpu.make_async_copy(blocks, blocks, send_sems.at[index]).wait()

    up = pltpu.make_async_remote_copy(
        src_ref=bases_ref.at[pl.ds(ROWS - 8, 8)],
        dst_ref=halo.at[0],
        send_sem=halo_send.at[0],
        recv_sem=halo_recv.at[0],
        device_id={"seq": lax.rem(me + 1, N_SEQ)},
        device_id_type=MESH,
    )
    down = pltpu.make_async_remote_copy(
        src_ref=bases_ref.at[pl.ds(0, 8)],
        dst_ref=halo.at[1],
        send_sem=halo_send.at[1],
        recv_sem=halo_recv.at[1],
        device_id={"seq": lax.rem(me + N_SEQ - 1, N_SEQ)},
        device_id_type=MESH,
    )
    up.start()
    down.start()
    send_all(0, lambda peer: tgt_out.at[peer // 2], tgt_in)
    tgt_in[pl.ds(me, 1)] = tgt_out[pl.ds(rho, 1)]

    lane = lax.broadcasted_iota(jnp.int32, (1, POOL), 1)

    def code_rows(start, count):
        total = ext[start : start + count, :] << 6
        here = ext[start : start + count, :]
        above = ext[start - 1 : start - 1 + count, :]
        below = ext[start + 1 : start + 1 + count, :]
        for shift in (1, 2):
            before = jnp.where(
                lane >= shift, pltpu.roll(here, shift, 1), pltpu.roll(above, shift, 1)
            )
            after = jnp.where(
                lane < POOL - shift,
                pltpu.roll(here, POOL - shift, 1),
                pltpu.roll(below, POOL - shift, 1),
            )
            total = total + (before << (3 * (2 - shift))) + (after << (3 * (2 + shift)))
        return total

    codes[0:240, :] = code_rows(16, 240)

    sub = lax.broadcasted_iota(jnp.int32, (8, POOL), 0)
    base_code = (sub & 3) + 1
    tap_shift = (sub >> 2) * 3
    zero_rows = jnp.zeros((8, POOL), F32)

    def stem_step(start):
        pieces = []
        for r in range(GROUP):
            code = jnp.broadcast_to(codes[pl.ds(start + r, 1), :], (8, POOL))
            taps = [
                jnp.where(((code >> (tap_shift + 6 * k)) & 7) == base_code, 1.0, 0.0).astype(F32)
                for k in range(3)
            ]
            pieces.append(jnp.concatenate(taps + [zero_rows], axis=0).astype(BF16))
        onehot = jnp.concatenate(pieces, axis=1)
        parts = []
        for n in range(STEM_CH // 256):
            stem = lax.dot_general(
                onehot,
                stem_w[:, 256 * n : 256 * n + 256].astype(BF16),
                (((0,), (0,)), ((), ())),
                preferred_element_type=F32,
            ).reshape(GROUP, POOL, 256)
            parts.append(
                jnp.maximum(gelu(jnp.max(stem, axis=1)), gelu(jnp.min(stem, axis=1)))
            )
        return jnp.concatenate(parts, axis=1).astype(BF16).astype(F32)

    def stem_body(g, carry):
        start = pl.multiple_of(g * GROUP, 8)
        pooled1[pl.ds(pl.multiple_of(16 + g * GROUP, 8), GROUP), :] = stem_step(start)
        return carry

    lax.fori_loop(0, 10, stem_body, 0)

    up.wait()
    down.wait()
    ext[0:8, :] = jnp.where(first, 0, halo[0] + 1)
    ext[8 + ROWS : 16 + ROWS, :] = jnp.where(last, 0, halo[1] + 1)
    codes[240:250, :] = code_rows(6, 10)
    codes[250:260, :] = code_rows(256, 10)
    codes[260:264, :] = jnp.zeros((4, POOL), jnp.int32)
    edge = stem_step(240)
    pooled1[6:16, :] = edge[0:10]
    pooled1[256:266, :] = edge[10:20]
    pooled1[6:8, :] = jnp.where(first, 0.0, edge[0:2])
    pooled1[264:266, :] = jnp.where(last, 0.0, edge[18:20])

    for k in range(5):
        lhs[:, STEM_CH * k : STEM_CH * k + STEM_CH] = pooled1[6 + k : 6 + k + ROWS, :].astype(BF16)

    for q in range(TILES):
        pltpu.make_async_copy(
            conv_ref.at[:, pl.ds(256 * q, 256)], conv_w.at[q], conv_sems.at[q]
        ).wait()

    def trunk_body(q, carry):
        trunk = jnp.dot(lhs[...], conv_w[q], preferred_element_type=F32)
        trunk = trunk.reshape(LOCAL, 16, 256)
        pooled2[q] = jnp.maximum(
            gelu(jnp.max(trunk, axis=1)), gelu(jnp.min(trunk, axis=1))
        )
        return carry

    lax.fori_loop(0, TILES, trunk_body, 0)

    sums = []
    squares = []
    for q in range(TILES):
        block = pooled2[q]
        sums.append(jnp.sum(block, axis=0, keepdims=True))
        squares.append(jnp.sum(block * block, axis=0, keepdims=True))
    for a in range(3):
        stat_out[a : a + 1, :] = jnp.concatenate(sums[2 * a : 2 * a + 2], axis=1)
        stat_out[4 + a : 5 + a, :] = jnp.concatenate(squares[2 * a : 2 * a + 2], axis=1)
    stat_out[3:4, :] = jnp.zeros((1, 512), F32)
    stat_out[7:8, :] = jnp.zeros((1, 512), F32)
    send_all(1, lambda peer: stat_out, stat_in)
    stat_in[pl.ds(me, 1)] = stat_out[...][None]

    zero_block = jnp.zeros((CH, CH), BF16)
    for a in range(4):
        for b in range(3):
            at = (3 * a + b) * CH
            near = pair_ref[(3 * a + b) * CH : (3 * a + b + 1) * CH, :] if a < 3 else zero_block
            far = (
                pair_ref[(3 * (a - 1) + b) * CH : (3 * (a - 1) + b + 1) * CH, :]
                if a > 0
                else zero_block
            )
            fwd_w[at : at + CH, :] = jnp.concatenate([near, far], axis=1)
            near = (
                pair_ref[(3 * (2 - a) + 2 - b) * CH : (3 * (2 - a) + 3 - b) * CH, :].T
                if a < 3
                else zero_block
            )
            far = (
                pair_ref[(3 * (3 - a) + 2 - b) * CH : (3 * (3 - a) + 3 - b) * CH, :].T
                if a > 0
                else zero_block
            )
            bwd_w[at : at + CH, :] = jnp.concatenate([near, far], axis=1)

    wait_recv(0, tgt_in)
    tgt_rows[...] = jnp.zeros_like(tgt_rows)
    for d in range(N_SEQ):
        tgt_rows[2 * d : 2 * d + 2, :] = tgt_in[d].astype(F32)
    tgt_t[...] = tgt_rows[...].T

    def chain_order(load):
        pieces = []
        for q in range(8):
            for s in range(4):
                pieces.append(load(q + 8 * s))
        return jnp.concatenate(pieces, axis=0)

    target = chain_order(lambda m: tgt_t[pl.ds(8 * m + 4 * half, 4), :])
    target = (target - 7.5) * 0.25

    zero_tile = jnp.zeros((16, CH), BF16)
    zero_row = jnp.zeros((160, CH), BF16)
    hid[0] = zero_row
    hid[33] = zero_row
    cgrad[0] = zero_row
    cgrad[33] = zero_row

    wait_recv(1, stat_in)
    total = jnp.sum(stat_in[...], axis=0)
    mean = total[0:4] / BINS
    var = total[4:8] / BINS - mean * mean
    scale = lax.rsqrt(var + 1e-05)
    normed = []
    for q in range(TILES):
        a, c = q // 2, 256 * (q % 2)
        normed.append(
            ((pooled2[q] - mean[a : a + 1, c : c + 256]) * scale[a : a + 1, c : c + 256]).astype(
                BF16
            )
        )
    normed = jnp.concatenate(normed, axis=1)
    proj = jnp.concatenate([row_proj_ref[...], col_proj_ref[...]], axis=1)
    emb = jnp.dot(normed, proj, preferred_element_type=F32).astype(BF16).astype(F32)
    rows_emb = emb[:, 0:CH]
    cols_emb = emb[:, CH : 2 * CH]
    for h in range(2):
        block = jnp.concatenate([cols_emb[4 * h : 4 * h + 4], cols_emb[8 + 4 * h : 12 + 4 * h]], 0)
        for r in range(8):
            emb_out[2 * r + h, 0:8, :] = block
            emb_out[2 * r + h, 8:9, :] = rows_emb[r : r + 1]
            emb_out[2 * r + h, 9:10, :] = rows_emb[r + 8 : r + 9]
            emb_out[2 * r + h, 10:16, :] = jnp.zeros((6, CH), F32)
    send_all(2, lambda peer: emb_out.at[peer], emb_in)
    emb_in[pl.ds(me, 1)] = emb_out[pl.ds(me, 1)]
    wait_recv(2, emb_in)

    for d in range(N_SEQ):
        rows_scr[2 * d : 2 * d + 2, :] = emb_in[d, 8:10, :]
    cols = chain_order(lambda m: emb_in[m // 2, 4 * (m % 2) : 4 * (m % 2) + 4, :])
    zero_four = jnp.zeros((4, CH), F32)

    def put_row(ref, index, values):
        ref[index, 16:144, :] = values.astype(BF16)
        ref[index, 0:16, :] = jnp.concatenate([zero_four, values[112:124]], axis=0).astype(BF16)
        ref[index, 144:160, :] = jnp.concatenate([values[4:16], zero_four], axis=0).astype(BF16)

    def hidden_body(u, carry):
        summed = cols + rows_scr[pl.ds(u, 1), :]
        value, slope = gelu_and_slope(summed)
        slope_scr[u] = slope
        put_row(hid, u + 1, value)
        return carry

    lax.fori_loop(0, 32, hidden_body, 0)

    out_scale = out_w_ref[...].astype(F32)
    chain_lane = lax.broadcasted_iota(jnp.int32, (CH, CH), 1)

    def conv_pairs(ref, weights, v, count):
        blocks = []
        for c in range(count):
            row = 2 * (v * count + c)
            blocks.append(
                jnp.concatenate(
                    [
                        ref[row + a, 16 * b : 16 * b + 128, :]
                        for a in range(4)
                        for b in range(3)
                    ],
                    axis=1,
                )
            )
        return jnp.dot(jnp.concatenate(blocks, axis=0), weights, preferred_element_type=F32)

    PAIRS = 4

    def forward_body(v, diff):
        conv = conv_pairs(hid, fwd_w[...], v, PAIRS)
        for c in range(PAIRS):
            for e in range(2):
                u = 2 * (v * PAIRS + c) + e
                out = conv[128 * c : 128 * c + 128, CH * e : CH * e + CH]
                value, slope = gelu_and_slope(out)
                summed = (hid[u + 1, 16:144, :].astype(F32) + value) * out_scale
                predicted = jnp.sum(summed, axis=1, keepdims=True)
                wanted = jnp.sum(
                    jnp.where(chain_lane == u, target, 0.0), axis=1, keepdims=True
                )
                direct = ((predicted - wanted) * 0.0625) * out_scale
                direct_scr[u] = direct
                put_row(cgrad, u + 1, direct * slope)
                diff = jnp.where(chain_lane == u, predicted, diff)
        return diff

    predicted = lax.fori_loop(0, 16 // PAIRS, forward_body, jnp.zeros((CH, CH), F32))

    pred_t[...] = jnp.zeros_like(pred_t)
    for q in range(8):
        for s in range(4):
            at = 16 * q + 4 * s
            pred_t[pl.ds(8 * (q + 8 * s) + 4 * half, 4), :] = predicted[at : at + 4]
    home = pred_t[...].T
    for d in range(N_SEQ):
        pred_out_s[d] = home[2 * d : 2 * d + 2]
    send_all(3, lambda peer: pred_out_s.at[peer], pred_in)
    pred_in[pl.ds(me, 1)] = pred_out_s[pl.ds(me, 1)]

    def backward_body(v, colsum):
        conv = conv_pairs(cgrad, bwd_w[...], v, PAIRS)
        for c in range(PAIRS):
            for e in range(2):
                u = 2 * (v * PAIRS + c) + e
                out = conv[128 * c : 128 * c + 128, CH * e : CH * e + CH]
                grad = (direct_scr[u] + out) * slope_scr[u]
                rowsum[pl.ds(u, 1), :] = jnp.sum(grad, axis=0, keepdims=True)
                colsum = colsum + grad
        return colsum

    colsum = lax.fori_loop(0, 16 // PAIRS, backward_body, jnp.zeros((CH, CH), F32))

    for d in range(N_SEQ):
        for e in range(2):
            m = 2 * d + e
            at = 16 * (m % 8) + 4 * (m // 8)
            part_out[d, 4 * e : 4 * e + 4, :] = colsum[at : at + 4]
        part_out[d, 8:10, :] = rowsum[2 * d : 2 * d + 2, :]
        part_out[d, 10:16, :] = jnp.zeros((6, CH), F32)
    send_all(4, lambda peer: part_out.at[peer], part_in)
    part_in[pl.ds(me, 1)] = part_out[pl.ds(me, 1)]

    wait_recv(3, pred_in)
    for r in range(8):
        both = pred_in[2 * r] + pred_in[2 * r + 1]
        pred_ref[r : r + 1, :] = both[0:1]
        pred_ref[r + 8 : r + 9, :] = both[1:2]

    wait_recv(4, part_in)
    col_halves = []
    for h in range(2):
        total = part_in[h, 0:8, :]
        for r in range(1, 8):
            total = total + part_in[2 * r + h, 0:8, :]
        col_halves.append(total)
    col_grad = jnp.concatenate(
        [
            col_halves[0][0:4],
            col_halves[1][0:4],
            col_halves[0][4:8],
            col_halves[1][4:8],
        ],
        axis=0,
    )
    row_pairs = [part_in[2 * r, 8:10, :] + part_in[2 * r + 1, 8:10, :] for r in range(8)]
    row_grad = jnp.concatenate(
        [pair[0:1] for pair in row_pairs] + [pair[1:2] for pair in row_pairs], axis=0
    )
    grads = jnp.concatenate([row_grad, col_grad], axis=1)
    high = grads.astype(BF16)
    rest = grads - high.astype(F32)
    middle = rest.astype(BF16)
    low = (rest - middle.astype(F32)).astype(BF16)
    stacked = jnp.concatenate([high, middle, low], axis=0)
    wide = lax.dot_general(
        stacked,
        jnp.concatenate([row_proj_ref[...], col_proj_ref[...]], axis=1),
        (((1,), (1,)), ((), ())),
        preferred_element_type=F32,
    )
    grad_ref[...] = (wide[32:48] + wide[16:32]) + wide[0:16]

    wait_send(0, tgt_in)
    wait_send(1, stat_in)
    wait_send(2, emb_in)
    wait_send(3, pred_in)
    wait_send(4, part_in)


def per_device(
    bases, stem_weight, conv_weight, row_proj, col_proj, pair_weight, out_weight, targets
):
    vmem = pl.BlockSpec(memory_space=pltpu.VMEM)
    return pl.pallas_call(
        fused,
        out_shape=(
            jax.ShapeDtypeStruct((LOCAL, BINS), F32),
            jax.ShapeDtypeStruct((LOCAL, TRUNK_CH), F32),
        ),
        in_specs=[vmem, vmem, pl.BlockSpec(memory_space=pl.ANY)] + [vmem] * 5,
        out_specs=(vmem, vmem),
        scratch_shapes=[
            pltpu.VMEM((2, 8, POOL), jnp.int32),
            pltpu.VMEM((ROWS + 16, POOL), jnp.int32),
            pltpu.VMEM((264, POOL), jnp.int32),
            pltpu.VMEM((32, STEM_CH), F32),
            pltpu.VMEM((ROWS + 16, STEM_CH), F32),
            pltpu.VMEM((ROWS, 5 * STEM_CH), BF16),
            pltpu.VMEM((TILES, 5 * STEM_CH, 256), BF16),
            pltpu.VMEM((TILES, LOCAL, 256), F32),
            pltpu.VMEM((8, 512), F32),
            pltpu.VMEM((N_SEQ, 8, 512), F32),
            pltpu.VMEM((N_SEQ, 16, CH), F32),
            pltpu.VMEM((N_SEQ, 16, CH), F32),
            pltpu.VMEM((8, 2, BINS), jnp.int32),
            pltpu.VMEM((N_SEQ, 2, BINS), jnp.int32),
            pltpu.VMEM((CH, BINS), F32),
            pltpu.VMEM((BINS, CH), F32),
            pltpu.VMEM((12 * CH, 2 * CH), BF16),
            pltpu.VMEM((12 * CH, 2 * CH), BF16),
            pltpu.VMEM((32, CH), F32),
            pltpu.VMEM((34, 160, CH), BF16),
            pltpu.VMEM((32, CH, CH), F32),
            pltpu.VMEM((32, CH, CH), F32),
            pltpu.VMEM((34, 160, CH), BF16),
            pltpu.VMEM((BINS, CH), F32),
            pltpu.VMEM((N_SEQ, 2, BINS), F32),
            pltpu.VMEM((N_SEQ, 2, BINS), F32),
            pltpu.VMEM((32, CH), F32),
            pltpu.VMEM((N_SEQ, 16, CH), F32),
            pltpu.VMEM((N_SEQ, 16, CH), F32),
            pltpu.SemaphoreType.DMA((TILES,)),
            pltpu.SemaphoreType.DMA((2,)),
            pltpu.SemaphoreType.DMA((2,)),
            pltpu.SemaphoreType.DMA((5,)),
            pltpu.SemaphoreType.DMA((5,)),
        ],
        compiler_params=pltpu.CompilerParams(
            collective_id=0, has_side_effects=True, vmem_limit_bytes=56 << 20
        ),
    )(
        bases.reshape(ROWS, POOL),
        stem_weight,
        conv_weight.reshape(5 * STEM_CH, TRUNK_CH),
        row_proj,
        col_proj,
        pair_weight.reshape(9 * CH, CH),
        out_weight.reshape(1, CH),
        targets,
    )


def solution(mesh):
    in_specs = (P(("dp", "seq")), P(), P(), P(), P(), P(), P(), P(("dp", "seq"), None))
    out_specs = (P(("dp", "seq"), None), P(("dp", "seq"), None))
    return jax.shard_map(
        per_device, mesh=mesh, in_specs=in_specs, out_specs=out_specs, check_vma=False
    )
```

```python
import functools
import math

import jax
import jax.numpy as jnp
from jax import lax
from jax.experimental import pallas as pl
from jax.experimental.pallas import tpu as pltpu
from jax.sharding import PartitionSpec as P

MESH = pl.DeviceIdType.MESH
F32 = jnp.float32
BF16 = jnp.bfloat16

N_SEQ = 16
STEM_CH = 768
TRUNK_CH = 1536
CH = 128
POOL = 128
ROWS = 256
BINS = 256
LOCAL = 16
GROUP = 24
TILES = TRUNK_CH // 256
C0 = math.sqrt(2.0 / math.pi)


def gelu(x):
    half = 0.5 * x
    return half + half * jnp.tanh(x * (C0 + (C0 * 0.044715) * (x * x)))


def gelu_and_slope(x):
    square = x * x
    a = 0.5 + 0.5 * jnp.tanh(x * (C0 + (C0 * 0.044715) * square))
    value = x * a
    slope = a + value * (1.0 - a) * (2.0 * C0 + (6.0 * C0 * 0.044715) * square)
    return value, slope


def fused(
    bases_ref,
    stem_ref,
    conv_ref,
    row_proj_ref,
    col_proj_ref,
    pair_hbm,
    out_w_ref,
    targets_ref,
    pred_ref,
    grad_ref,
    halo,
    ext,
    codes,
    stem_w,
    pooled1,
    lhs,
    conv_w,
    pooled2,
    proj,
    pair_ref,
    stat_all,
    stat_out,
    stat_in,
    late_out,
    late_in,
    emb_out,
    emb_in,
    tgt_rows,
    tgt_t,
    fwd_w,
    bwd_w,
    rows_scr,
    hid,
    slope_scr,
    direct_scr,
    cgrad,
    pred_t,
    rowsum,
    part_out,
    part_in,
    conv_sems,
    weight_sems,
    halo_send,
    halo_recv,
    send_sems,
    recv_sems,
):
    me = lax.axis_index("seq")
    rho = me // 2
    half = me % 2
    first = me == 0
    last = me == N_SEQ - 1

    conv_copies = [
        pltpu.make_async_copy(
            conv_ref.at[:, pl.ds(256 * q, 256)], conv_w.at[q], conv_sems.at[q]
        )
        for q in range(TILES)
    ]
    weight_copies = [
        pltpu.make_async_copy(row_proj_ref, proj.at[:, pl.ds(0, CH)], weight_sems.at[0]),
        pltpu.make_async_copy(col_proj_ref, proj.at[:, pl.ds(CH, CH)], weight_sems.at[1]),
        pltpu.make_async_copy(pair_hbm, pair_ref, weight_sems.at[2]),
    ]
    for copy in conv_copies + weight_copies:
        copy.start()

    barrier = pltpu.get_barrier_semaphore()

    def greet(k, carry):
        peer = lax.rem(me + k, N_SEQ)
        pl.semaphore_signal(barrier, inc=1, device_id={"seq": peer}, device_id_type=MESH)
        return carry

    lax.fori_loop(1, N_SEQ, greet, 0)

    ext[...] = jnp.zeros_like(ext)
    ext[8 : 8 + ROWS, :] = bases_ref[...] + 1
    stem_w[...] = jnp.zeros_like(stem_w)
    stem_w[0:20, :] = stem_ref[...].astype(F32)

    def send_all(index, source_of, landing):
        def one(k, carry):
            peer = lax.rem(me + k, N_SEQ)
            pltpu.make_async_remote_copy(
                src_ref=source_of(peer),
                dst_ref=landing.at[me],
                send_sem=send_sems.at[index],
                recv_sem=recv_sems.at[index],
                device_id={"seq": peer},
                device_id_type=MESH,
            ).start()
            return carry

        lax.fori_loop(1, N_SEQ, one, 0)

    def wait_recv(index, landing):
        blocks = landing.at[pl.ds(0, N_SEQ - 1)]
        pltpu.make_async_copy(blocks, blocks, recv_sems.at[index]).wait()

    def wait_send(index, landing):
        blocks = landing.at[pl.ds(0, N_SEQ - 1)]
        pltpu.make_async_copy(blocks, blocks, send_sems.at[index]).wait()

    lane = lax.broadcasted_iota(jnp.int32, (1, POOL), 1)

    def code_rows(start, count):
        total = ext[start : start + count, :] << 6
        here = ext[start : start + count, :]
        above = ext[start - 1 : start - 1 + count, :]
        below = ext[start + 1 : start + 1 + count, :]
        for shift in (1, 2):
            before = jnp.where(
                lane >= shift, pltpu.roll(here, shift, 1), pltpu.roll(above, shift, 1)
            )
            after = jnp.where(
                lane < POOL - shift,
                pltpu.roll(here, POOL - shift, 1),
                pltpu.roll(below, POOL - shift, 1),
            )
            total = total + (before << (3 * (2 - shift))) + (after << (3 * (2 + shift)))
        return total

    codes[0:240, :] = code_rows(16, 240)

    sub = lax.broadcasted_iota(jnp.int32, (8, POOL), 0)
    base_code = (sub & 3) + 1
    tap_shift = (sub >> 2) * 3
    zero_rows = jnp.zeros((8, POOL), F32)

    def stem_step(start):
        pieces = []
        for r in range(GROUP):
            code = jnp.broadcast_to(codes[pl.ds(start + r, 1), :], (8, POOL))
            taps = [
                jnp.where(((code >> (tap_shift + 6 * k)) & 7) == base_code, 1.0, 0.0).astype(F32)
                for k in range(3)
            ]
            pieces.append(jnp.concatenate(taps + [zero_rows], axis=0).astype(BF16))
        onehot = jnp.concatenate(pieces, axis=1)
        parts = []
        for n in range(STEM_CH // 256):
            stem = lax.dot_general(
                onehot,
                stem_w[:, 256 * n : 256 * n + 256].astype(BF16),
                (((0,), (0,)), ((), ())),
                preferred_element_type=F32,
            ).reshape(GROUP, POOL, 256)
            parts.append(
                jnp.maximum(gelu(jnp.max(stem, axis=1)), gelu(jnp.min(stem, axis=1)))
            )
        return jnp.concatenate(parts, axis=1).astype(BF16).astype(F32)

    up = pltpu.make_async_remote_copy(
        src_ref=bases_ref.at[pl.ds(ROWS - 8, 8)],
        dst_ref=halo.at[0],
        send_sem=halo_send.at[0],
        recv_sem=halo_recv.at[0],
        device_id={"seq": lax.rem(me + 1, N_SEQ)},
        device_id_type=MESH,
    )
    down = pltpu.make_async_remote_copy(
        src_ref=bases_ref.at[pl.ds(0, 8)],
        dst_ref=halo.at[1],
        send_sem=halo_send.at[1],
        recv_sem=halo_recv.at[1],
        device_id={"seq": lax.rem(me + N_SEQ - 1, N_SEQ)},
        device_id_type=MESH,
    )

    def stem_body(g, carry):
        @pl.when(g == 2)
        def _():
            pl.semaphore_wait(barrier, N_SEQ - 1)
            up.start()
            down.start()

        @pl.when(g == 10)
        def _():
            up.wait()
            down.wait()
            ext[0:8, :] = jnp.where(first, 0, halo[0] + 1)
            ext[8 + ROWS : 16 + ROWS, :] = jnp.where(last, 0, halo[1] + 1)
            codes[240:250, :] = code_rows(6, 10)
            codes[250:260, :] = code_rows(256, 10)
            codes[260:264, :] = jnp.zeros((4, POOL), jnp.int32)

        start = pl.multiple_of(g * GROUP, 8)
        pooled1[pl.ds(pl.multiple_of(16 + g * GROUP, 8), GROUP), :] = stem_step(start)
        return carry

    lax.fori_loop(0, 11, stem_body, 0)
    edge = pooled1[256:280, :]
    pooled1[6:16, :] = edge[0:10]
    pooled1[256:266, :] = edge[10:20]
    pooled1[6:8, :] = jnp.where(first, 0.0, edge[0:2])
    pooled1[264:266, :] = jnp.where(last, 0.0, edge[18:20])

    for k in range(5):
        lhs[:, STEM_CH * k : STEM_CH * k + STEM_CH] = pooled1[6 + k : 6 + k + ROWS, :].astype(BF16)

    for copy in conv_copies:
        copy.wait()

    def trunk_tile(q):
        trunk = jnp.dot(lhs[...], conv_w[q], preferred_element_type=F32)
        trunk = trunk.reshape(LOCAL, 16, 256)
        block = jnp.maximum(gelu(jnp.max(trunk, axis=1)), gelu(jnp.min(trunk, axis=1)))
        pooled2[q] = block
        total = jnp.sum(block, axis=0, keepdims=True)
        return total, jnp.sum(block * block, axis=0, keepdims=True)

    def tile(q, carry):
        total, square = trunk_tile(q)
        stat_all[pl.ds(q, 1), :] = total
        stat_all[pl.ds(8 + q, 1), :] = square

        @pl.when(q == 3)
        def _():
            stat_out[0:4, :] = stat_all[0:4, :]
            stat_out[4:8, :] = stat_all[8:12, :]
            send_all(0, lambda peer: stat_out, stat_in)

        return carry

    lax.fori_loop(0, TILES, tile, 0)
    stat_in[pl.ds(me, 1)] = stat_out[...][None]
    for r in range(8):
        late_out[r, 0:2, :] = stat_all[4:6, :]
        late_out[r, 2:4, :] = stat_all[12:14, :]
    for r in range(8):
        for e in range(2):
            late_out[r, 4 + e : 5 + e, :] = targets_ref[r + 8 * e : r + 8 * e + 1, :].astype(F32)
        late_out[r, 6:8, :] = jnp.zeros((2, 256), F32)
    send_all(1, lambda peer: late_out.at[peer // 2], late_in)
    late_in[pl.ds(me, 1)] = late_out[pl.ds(rho, 1)]

    for copy in weight_copies:
        copy.wait()
    zero_block = jnp.zeros((CH, CH), BF16)
    for a in range(4):
        for b in range(3):
            at = (3 * a + b) * CH
            near = pair_ref[(3 * a + b) * CH : (3 * a + b + 1) * CH, :] if a < 3 else zero_block
            far = (
                pair_ref[(3 * (a - 1) + b) * CH : (3 * (a - 1) + b + 1) * CH, :]
                if a > 0
                else zero_block
            )
            fwd_w[at : at + CH, :] = jnp.concatenate([near, far], axis=1)
            near = (
                pair_ref[(3 * (2 - a) + 2 - b) * CH : (3 * (2 - a) + 3 - b) * CH, :].T
                if a < 3
                else zero_block
            )
            far = (
                pair_ref[(3 * (3 - a) + 2 - b) * CH : (3 * (3 - a) + 3 - b) * CH, :].T
                if a > 0
                else zero_block
            )
            bwd_w[at : at + CH, :] = jnp.concatenate([near, far], axis=1)

    zero_row = jnp.zeros((160, CH), BF16)
    hid[0] = zero_row
    hid[33] = zero_row
    cgrad[0] = zero_row
    cgrad[33] = zero_row

    wait_recv(0, stat_in)
    early = jnp.sum(stat_in[...], axis=0)
    wait_recv(1, late_in)
    late = jnp.sum(late_in[...], axis=0)
    mean = jnp.concatenate([early[0:4], late[0:2]], axis=0) / BINS
    var = jnp.concatenate([early[4:8], late[2:4]], axis=0) / BINS - mean * mean
    scale = lax.rsqrt(var + 1e-05)
    normed = jnp.concatenate(
        [
            ((pooled2[q] - mean[q : q + 1]) * scale[q : q + 1]).astype(BF16)
            for q in range(TILES)
        ],
        axis=1,
    )
    emb = jnp.dot(normed, proj[...], preferred_element_type=F32).astype(BF16).astype(F32)
    rows_emb = emb[:, 0:CH]
    cols_emb = emb[:, CH : 2 * CH]
    for h in range(2):
        block = jnp.concatenate([cols_emb[4 * h : 4 * h + 4], cols_emb[8 + 4 * h : 12 + 4 * h]], 0)
        for r in range(8):
            emb_out[2 * r + h, 0:8, :] = block
            emb_out[2 * r + h, 8:9, :] = rows_emb[r : r + 1]
            emb_out[2 * r + h, 9:10, :] = rows_emb[r + 8 : r + 9]
            emb_out[2 * r + h, 10:16, :] = jnp.zeros((6, CH), F32)
    send_all(2, lambda peer: emb_out.at[peer], emb_in)
    emb_in[pl.ds(me, 1)] = emb_out[pl.ds(me, 1)]

    tgt_rows[...] = jnp.zeros_like(tgt_rows)
    for d in range(N_SEQ):
        tgt_rows[2 * d : 2 * d + 2, :] = late_in[d, 4:6, :]
    tgt_t[...] = tgt_rows[...].T

    def chain_order(load):
        pieces = []
        for q in range(8):
            for s in range(4):
                pieces.append(load(q + 8 * s))
        return jnp.concatenate(pieces, axis=0)

    target = chain_order(lambda m: tgt_t[pl.ds(8 * m + 4 * half, 4), :])
    target = (target - 7.5) * 0.25

    wait_recv(2, emb_in)

    for d in range(N_SEQ):
        rows_scr[2 * d : 2 * d + 2, :] = emb_in[d, 8:10, :]
    cols = chain_order(lambda m: emb_in[m // 2, 4 * (m % 2) : 4 * (m % 2) + 4, :])
    zero_four = jnp.zeros((4, CH), F32)

    def put_row(ref, index, values):
        ref[index, 16:144, :] = values.astype(BF16)
        ref[index, 0:16, :] = jnp.concatenate([zero_four, values[112:124]], axis=0).astype(BF16)
        ref[index, 144:160, :] = jnp.concatenate([values[4:16], zero_four], axis=0).astype(BF16)

    def hidden_body(u, carry):
        summed = cols + rows_scr[pl.ds(u, 1), :]
        value, slope = gelu_and_slope(summed)
        slope_scr[u] = slope
        put_row(hid, u + 1, value)
        return carry

    lax.fori_loop(0, 32, hidden_body, 0, unroll=4)

    out_scale = out_w_ref[...].astype(F32)
    small_scale = out_scale * (1.0 / math.sqrt(BINS))
    chain_lane = lax.broadcasted_iota(jnp.int32, (CH, CH), 1)

    def conv_pairs(ref, weights, v, count):
        blocks = []
        for c in range(count):
            row = 2 * (v * count + c)
            blocks.append(
                jnp.concatenate(
                    [
                        ref[row + a, 16 * b : 16 * b + 128, :]
                        for a in range(4)
                        for b in range(3)
                    ],
                    axis=1,
                )
            )
        return jnp.dot(jnp.concatenate(blocks, axis=0), weights, preferred_element_type=F32)

    PAIRS = 8

    def forward_body(v, diff):
        conv = conv_pairs(hid, fwd_w[...], v, PAIRS)
        for c in range(PAIRS):
            for e in range(2):
                u = 2 * (v * PAIRS + c) + e
                out = conv[128 * c : 128 * c + 128, CH * e : CH * e + CH]
                value, slope = gelu_and_slope(out)
                summed = (hid[u + 1, 16:144, :].astype(F32) + value) * out_scale
                summed = summed - jnp.where(chain_lane == u, target, 0.0)
                error = jnp.sum(summed, axis=1, keepdims=True)
                direct = error * small_scale
                direct_scr[u] = direct
                put_row(cgrad, u + 1, direct * slope)
                diff = jnp.where(chain_lane == u, error, diff)
        return diff

    errors = lax.fori_loop(0, 16 // PAIRS, forward_body, jnp.zeros((CH, CH), F32))
    predicted = errors + target

    def backward_body(v, colsum):
        conv = conv_pairs(cgrad, bwd_w[...], v, PAIRS)
        for c in range(PAIRS):
            for e in range(2):
                u = 2 * (v * PAIRS + c) + e
                out = conv[128 * c : 128 * c + 128, CH * e : CH * e + CH]
                grad = (direct_scr[u] + out) * slope_scr[u]
                rowsum[pl.ds(u, 1), :] = jnp.sum(grad, axis=0, keepdims=True)
                colsum = colsum + grad
        return colsum

    colsum = lax.fori_loop(0, 16 // PAIRS, backward_body, jnp.zeros((CH, CH), F32))

    pred_t[...] = jnp.zeros_like(pred_t)
    for q in range(8):
        for s in range(4):
            at = 16 * q + 4 * s
            pred_t[pl.ds(8 * (q + 8 * s) + 4 * half, 4), :] = predicted[at : at + 4]
    home = pred_t[...].T
    for d in range(N_SEQ):
        for e in range(2):
            m = 2 * d + e
            at = 16 * (m % 8) + 4 * (m // 8)
            part_out[d, 4 * e : 4 * e + 4, :] = colsum[at : at + 4]
            part_out[d, 10 + e : 11 + e, :] = home[m : m + 1, 0:CH]
            part_out[d, 12 + e : 13 + e, :] = home[m : m + 1, CH : 2 * CH]
        part_out[d, 8:10, :] = rowsum[2 * d : 2 * d + 2, :]
        part_out[d, 14:16, :] = jnp.zeros((2, CH), F32)
    send_all(3, lambda peer: part_out.at[peer], part_in)
    part_in[pl.ds(me, 1)] = part_out[pl.ds(me, 1)]

    wait_recv(3, part_in)
    for r in range(8):
        both = part_in[2 * r, 10:14, :] + part_in[2 * r + 1, 10:14, :]
        for e in range(2):
            pred_ref[r + 8 * e : r + 8 * e + 1, 0:CH] = both[e : e + 1]
            pred_ref[r + 8 * e : r + 8 * e + 1, CH : 2 * CH] = both[2 + e : 3 + e]
    col_halves = []
    for h in range(2):
        total = part_in[h, 0:8, :]
        for r in range(1, 8):
            total = total + part_in[2 * r + h, 0:8, :]
        col_halves.append(total)
    col_grad = jnp.concatenate(
        [
            col_halves[0][0:4],
            col_halves[1][0:4],
            col_halves[0][4:8],
            col_halves[1][4:8],
        ],
        axis=0,
    )
    row_pairs = [part_in[2 * r, 8:10, :] + part_in[2 * r + 1, 8:10, :] for r in range(8)]
    row_grad = jnp.concatenate(
        [pair[0:1] for pair in row_pairs] + [pair[1:2] for pair in row_pairs], axis=0
    )
    grads = jnp.concatenate([row_grad, col_grad], axis=1)
    high = grads.astype(BF16)
    rest = grads - high.astype(F32)
    middle = rest.astype(BF16)
    low = (rest - middle.astype(F32)).astype(BF16)
    stacked = jnp.concatenate([high, middle, low], axis=0)
    wide = lax.dot_general(
        stacked,
        proj[...],
        (((1,), (1,)), ((), ())),
        preferred_element_type=F32,
    )
    grad_ref[...] = (wide[32:48] + wide[16:32]) + wide[0:16]

    wait_send(0, stat_in)
    wait_send(1, late_in)
    wait_send(2, emb_in)
    wait_send(3, part_in)


def per_device(
    bases, stem_weight, conv_weight, row_proj, col_proj, pair_weight, out_weight, targets
):
    vmem = pl.BlockSpec(memory_space=pltpu.VMEM)
    hbm = pl.BlockSpec(memory_space=pl.ANY)
    return pl.pallas_call(
        fused,
        out_shape=(
            jax.ShapeDtypeStruct((LOCAL, BINS), F32),
            jax.ShapeDtypeStruct((LOCAL, TRUNK_CH), F32),
        ),
        in_specs=[vmem, vmem, hbm, hbm, hbm, hbm, vmem, vmem],
        out_specs=(vmem, vmem),
        scratch_shapes=[
            pltpu.VMEM((2, 8, POOL), jnp.int32),
            pltpu.VMEM((ROWS + 16, POOL), jnp.int32),
            pltpu.VMEM((264, POOL), jnp.int32),
            pltpu.VMEM((32, STEM_CH), F32),
            pltpu.VMEM((ROWS + 24, STEM_CH), F32),
            pltpu.VMEM((ROWS, 5 * STEM_CH), BF16),
            pltpu.VMEM((TILES, 5 * STEM_CH, 256), BF16),
            pltpu.VMEM((TILES, LOCAL, 256), F32),
            pltpu.VMEM((TRUNK_CH, 2 * CH), BF16),
            pltpu.VMEM((9 * CH, CH), BF16),
            pltpu.VMEM((16, 256), F32),
            pltpu.VMEM((8, 256), F32),
            pltpu.VMEM((N_SEQ, 8, 256), F32),
            pltpu.VMEM((8, 8, 256), F32),
            pltpu.VMEM((N_SEQ, 8, 256), F32),
            pltpu.VMEM((N_SEQ, 16, CH), F32),
            pltpu.VMEM((N_SEQ, 16, CH), F32),
            pltpu.VMEM((CH, BINS), F32),
            pltpu.VMEM((BINS, CH), F32),
            pltpu.VMEM((12 * CH, 2 * CH), BF16),
            pltpu.VMEM((12 * CH, 2 * CH), BF16),
            pltpu.VMEM((32, CH), F32),
            pltpu.VMEM((34, 160, CH), BF16),
            pltpu.VMEM((32, CH, CH), F32),
            pltpu.VMEM((32, CH, CH), F32),
            pltpu.VMEM((34, 160, CH), BF16),
            pltpu.VMEM((BINS, CH), F32),
            pltpu.VMEM((32, CH), F32),
            pltpu.VMEM((N_SEQ, 16, CH), F32),
            pltpu.VMEM((N_SEQ, 16, CH), F32),
            pltpu.SemaphoreType.DMA((TILES,)),
            pltpu.SemaphoreType.DMA((3,)),
            pltpu.SemaphoreType.DMA((2,)),
            pltpu.SemaphoreType.DMA((2,)),
            pltpu.SemaphoreType.DMA((4,)),
            pltpu.SemaphoreType.DMA((4,)),
        ],
        compiler_params=pltpu.CompilerParams(
            collective_id=0, has_side_effects=True, vmem_limit_bytes=56 << 20
        ),
    )(
        bases.reshape(ROWS, POOL),
        stem_weight,
        conv_weight.reshape(5 * STEM_CH, TRUNK_CH),
        row_proj,
        col_proj,
        pair_weight.reshape(9 * CH, CH),
        out_weight.reshape(1, CH),
        targets,
    )


def solution(mesh):
    in_specs = (P(("dp", "seq")), P(), P(), P(), P(), P(), P(), P(("dp", "seq"), None))
    out_specs = (P(("dp", "seq"), None), P(("dp", "seq"), None))
    return jax.shard_map(
        per_device, mesh=mesh, in_specs=in_specs, out_specs=out_specs, check_vma=False
    )
```

```python
import functools
import math

import jax
import jax.numpy as jnp
from jax import lax
from jax.experimental import pallas as pl
from jax.experimental.pallas import tpu as pltpu
from jax.sharding import PartitionSpec as P

MESH = pl.DeviceIdType.MESH
FAR_FIRST = sorted(
    [(z, x, c) for z in range(2) for x in range(4) for c in range(2) if (z, x, c) != (0, 0, 0)],
    key=lambda d: -(d[0] + min(d[1], 4 - d[1]) + 0.1 * d[2]),
)
F32 = jnp.float32
BF16 = jnp.bfloat16

N_SEQ = 16
STEM_CH = 768
TRUNK_CH = 1536
CH = 128
POOL = 128
ROWS = 256
BINS = 256
LOCAL = 16
OFF = 32
GROUP = 24
TILES = TRUNK_CH // 256
C0 = math.sqrt(2.0 / math.pi)


def gelu(x):
    half = 0.5 * x
    return half + half * jnp.tanh(x * (C0 + (C0 * 0.044715) * (x * x)))


def gelu_and_slope(x):
    square = x * x
    a = 0.5 + 0.5 * jnp.tanh(x * (C0 + (C0 * 0.044715) * square))
    value = x * a
    slope = a + value * (1.0 - a) * (2.0 * C0 + (6.0 * C0 * 0.044715) * square)
    return value, slope


def fused(
    bases_hbm,
    stem_hbm,
    conv_ref,
    row_proj_ref,
    col_proj_ref,
    pair_hbm,
    out_w_hbm,
    targets_hbm,
    pred_ref,
    grad_ref,
    bases_ref,
    stem_ref,
    out_w_ref,
    targets_ref,
    halo,
    ext,
    codes,
    stem_w,
    onehot,
    extremes,
    pooled1,
    lhs,
    conv_w,
    pooled2,
    proj,
    pair_ref,
    stat_all,
    stat_out,
    stat_in,
    late_out,
    late_in,
    emb_out,
    emb_in,
    tgt_rows,
    tgt_t,
    fwd_w,
    bwd_w,
    rows_scr,
    hid,
    slope_scr,
    direct_scr,
    cgrad,
    pred_t,
    rowsum,
    part_out,
    part_in,
    input_sems,
    conv_sems,
    weight_sems,
    halo_send,
    halo_recv,
    send_sems,
    recv_sems,
):
    me = lax.axis_index("seq")
    rho = me // 2
    half = me % 2
    z, x, core = me // 8, lax.rem(me // 2, 4), half
    first = me == 0
    last = me == N_SEQ - 1

    input_copies = [
        pltpu.make_async_copy(bases_hbm, bases_ref, input_sems.at[0]),
        pltpu.make_async_copy(stem_hbm, stem_ref, input_sems.at[1]),
        pltpu.make_async_copy(out_w_hbm, out_w_ref, input_sems.at[2]),
        pltpu.make_async_copy(targets_hbm, targets_ref, input_sems.at[3]),
    ]
    for copy in input_copies:
        copy.start()
    conv_copies = [
        pltpu.make_async_copy(
            conv_ref.at[:, pl.ds(256 * q, 256)], conv_w.at[q], conv_sems.at[q]
        )
        for q in range(TILES)
    ]
    weight_copies = [
        pltpu.make_async_copy(row_proj_ref, proj.at[:, pl.ds(0, CH)], weight_sems.at[0]),
        pltpu.make_async_copy(col_proj_ref, proj.at[:, pl.ds(CH, CH)], weight_sems.at[1]),
        pltpu.make_async_copy(pair_hbm, pair_ref, weight_sems.at[2]),
    ]

    barrier = pltpu.get_barrier_semaphore()

    def greet(k, carry):
        peer = lax.rem(me + k, N_SEQ)
        pl.semaphore_signal(barrier, inc=1, device_id={"seq": peer}, device_id_type=MESH)
        return carry

    lax.fori_loop(1, N_SEQ, greet, 0)

    ext[...] = jnp.zeros_like(ext)
    for copy in input_copies:
        copy.wait()
    ext[8 : 8 + ROWS, :] = bases_ref[...] + 1
    stem_w[...] = jnp.zeros_like(stem_w)
    stem_w[0:20, :] = stem_ref[...].astype(F32)

    def send_all(index, source_of, landing):
        for dz, dx, dc in FAR_FIRST:
            peer = 8 * lax.rem(z + dz, 2) + 2 * lax.rem(x + dx, 4) + lax.rem(core + dc, 2)
            pltpu.make_async_remote_copy(
                src_ref=source_of(peer),
                dst_ref=landing.at[me],
                send_sem=send_sems.at[index],
                recv_sem=recv_sems.at[index],
                device_id={"seq": peer},
                device_id_type=MESH,
            ).start()

    def wait_recv(index, landing):
        blocks = landing.at[pl.ds(0, N_SEQ - 1)]
        pltpu.make_async_copy(blocks, blocks, recv_sems.at[index]).wait()

    def wait_send(index, landing):
        blocks = landing.at[pl.ds(0, N_SEQ - 1)]
        pltpu.make_async_copy(blocks, blocks, send_sems.at[index]).wait()

    lane = lax.broadcasted_iota(jnp.int32, (1, POOL), 1)

    def code_rows(start, count):
        total = ext[start : start + count, :] << 6
        here = ext[start : start + count, :]
        above = ext[start - 1 : start - 1 + count, :]
        below = ext[start + 1 : start + 1 + count, :]
        for shift in (1, 2):
            before = jnp.where(
                lane >= shift, pltpu.roll(here, shift, 1), pltpu.roll(above, shift, 1)
            )
            after = jnp.where(
                lane < POOL - shift,
                pltpu.roll(here, POOL - shift, 1),
                pltpu.roll(below, POOL - shift, 1),
            )
            total = total + (before << (3 * (2 - shift))) + (after << (3 * (2 + shift)))
        return total

    codes[0:240, :] = code_rows(16, 240)

    sub = lax.broadcasted_iota(jnp.int32, (8, POOL), 0)
    base_code = (sub & 3) + 1
    tap_shift = (sub >> 2) * 3
    zero_rows = jnp.zeros((8, POOL), F32)

    def onehot_rows(start, r):
        code = jnp.broadcast_to(codes[pl.ds(start + r, 1), :], (8, POOL))
        taps = [
            jnp.where(((code >> (tap_shift + 6 * k)) & 7) == base_code, 1.0, 0.0).astype(F32)
            for k in range(3)
        ]
        return jnp.concatenate(taps + [zero_rows], axis=0).astype(BF16).T

    def pooled_rows():
        values = jnp.maximum(gelu(extremes[0]), gelu(extremes[1]))
        return values.astype(BF16).astype(F32)

    up = pltpu.make_async_remote_copy(
        src_ref=bases_ref.at[pl.ds(ROWS - 8, 8)],
        dst_ref=halo.at[0],
        send_sem=halo_send.at[0],
        recv_sem=halo_recv.at[0],
        device_id={"seq": lax.rem(me + 1, N_SEQ)},
        device_id_type=MESH,
    )
    down = pltpu.make_async_remote_copy(
        src_ref=bases_ref.at[pl.ds(0, 8)],
        dst_ref=halo.at[1],
        send_sem=halo_send.at[1],
        recv_sem=halo_recv.at[1],
        device_id={"seq": lax.rem(me + N_SEQ - 1, N_SEQ)},
        device_id_type=MESH,
    )

    def first_onehot(r, carry):
        onehot[0, pl.ds(pl.multiple_of(POOL * r, POOL), POOL), :] = onehot_rows(0, r)
        return carry

    lax.fori_loop(0, GROUP, first_onehot, 0, unroll=12)
    extremes[...] = jnp.zeros_like(extremes)

    def stem_body(g, carry):
        @pl.when(g == 2)
        def _():
            pl.semaphore_wait(barrier, N_SEQ - 1)
            up.start()
            down.start()
            for copy in conv_copies + weight_copies:
                copy.start()

        @pl.when(g == 9)
        def _():
            up.wait()
            down.wait()
            ext[0:8, :] = jnp.where(first, 0, halo[0] + 1)
            ext[8 + ROWS : 16 + ROWS, :] = jnp.where(last, 0, halo[1] + 1)
            codes[240:250, :] = code_rows(6, 10)
            codes[250:260, :] = code_rows(256, 10)
            codes[260:264, :] = jnp.zeros((4, POOL), jnp.int32)

        slot = lax.rem(g, 2)
        pooled1[pl.ds(pl.multiple_of(OFF - 16 + g * GROUP, 8), GROUP), :] = pooled_rows()
        for n in range(STEM_CH // 256):
            stem = jnp.dot(
                onehot[slot],
                stem_w[:, 256 * n : 256 * n + 256].astype(BF16),
                preferred_element_type=F32,
            ).reshape(GROUP, POOL, 256)
            extremes[0, :, 256 * n : 256 * n + 256] = jnp.max(stem, axis=1)
            extremes[1, :, 256 * n : 256 * n + 256] = jnp.min(stem, axis=1)
        start = pl.multiple_of(jnp.minimum(g + 1, 10) * GROUP, 8)
        for r in range(GROUP):
            onehot[1 - slot, POOL * r : POOL * r + POOL, :] = onehot_rows(start, r)
        return carry

    lax.fori_loop(0, 11, stem_body, 0)
    edge = pooled_rows()
    pooled1[OFF - 2 : OFF + 8, :] = edge[0:10]
    pooled1[OFF + 248 : OFF + 258, :] = edge[10:20]
    pooled1[OFF - 2 : OFF, :] = jnp.where(first, 0.0, edge[0:2])
    pooled1[OFF + 256 : OFF + 258, :] = jnp.where(last, 0.0, edge[18:20])

    for k in range(5):
        lhs[:, STEM_CH * k : STEM_CH * k + STEM_CH] = pooled1[OFF - 2 + k : OFF - 2 + k + ROWS, :].astype(BF16)

    for copy in conv_copies:
        copy.wait()

    def trunk_tile(q):
        trunk = jnp.dot(lhs[...], conv_w[q], preferred_element_type=F32)
        trunk = trunk.reshape(LOCAL, 16, 256)
        block = jnp.maximum(gelu(jnp.max(trunk, axis=1)), gelu(jnp.min(trunk, axis=1)))
        pooled2[q] = block
        total = jnp.sum(block, axis=0, keepdims=True)
        return total, jnp.sum(block * block, axis=0, keepdims=True)

    for q in range(TILES):
        total, square = trunk_tile(q)
        stat_all[q : q + 1, :] = total
        stat_all[8 + q : 9 + q, :] = square
        if q == 3:
            stat_out[0:4, :] = stat_all[0:4, :]
            stat_out[4:8, :] = stat_all[8:12, :]
            send_all(0, lambda peer: stat_out, stat_in)
    stat_in[pl.ds(me, 1)] = stat_out[...][None]
    for r in range(8):
        late_out[r, 0:2, :] = stat_all[4:6, :]
        late_out[r, 2:4, :] = stat_all[12:14, :]
    for r in range(8):
        for e in range(2):
            late_out[r, 4 + e : 5 + e, :] = targets_ref[r + 8 * e : r + 8 * e + 1, :].astype(F32)
        late_out[r, 6:8, :] = jnp.zeros((2, 256), F32)
    send_all(1, lambda peer: late_out.at[peer // 2], late_in)
    late_in[pl.ds(me, 1)] = late_out[pl.ds(rho, 1)]

    for copy in weight_copies:
        copy.wait()
    zero_block = jnp.zeros((CH, CH), BF16)
    for a in range(4):
        for b in range(3):
            at = (3 * a + b) * CH
            near = pair_ref[(3 * a + b) * CH : (3 * a + b + 1) * CH, :] if a < 3 else zero_block
            far = (
                pair_ref[(3 * (a - 1) + b) * CH : (3 * (a - 1) + b + 1) * CH, :]
                if a > 0
                else zero_block
            )
            fwd_w[at : at + CH, :] = jnp.concatenate([near, far], axis=1)
            near = (
                pair_ref[(3 * (2 - a) + 2 - b) * CH : (3 * (2 - a) + 3 - b) * CH, :].T
                if a < 3
                else zero_block
            )
            far = (
                pair_ref[(3 * (3 - a) + 2 - b) * CH : (3 * (3 - a) + 3 - b) * CH, :].T
                if a > 0
                else zero_block
            )
            bwd_w[at : at + CH, :] = jnp.concatenate([near, far], axis=1)

    zero_row = jnp.zeros((160, CH), BF16)
    hid[0] = zero_row
    hid[33] = zero_row
    cgrad[0] = zero_row
    cgrad[33] = zero_row

    wait_recv(0, stat_in)
    early = jnp.sum(stat_in[...], axis=0)
    wait_recv(1, late_in)
    late = jnp.sum(late_in[...], axis=0)
    mean = jnp.concatenate([early[0:4], late[0:2]], axis=0) / BINS
    var = jnp.concatenate([early[4:8], late[2:4]], axis=0) / BINS - mean * mean
    scale = lax.rsqrt(var + 1e-05)
    normed = jnp.concatenate(
        [
            ((pooled2[q] - mean[q : q + 1]) * scale[q : q + 1]).astype(BF16)
            for q in range(TILES)
        ],
        axis=1,
    )
    emb = jnp.dot(normed, proj[...], preferred_element_type=F32).astype(BF16).astype(F32)
    rows_emb = emb[:, 0:CH]
    cols_emb = emb[:, CH : 2 * CH]
    for h in range(2):
        block = jnp.concatenate([cols_emb[4 * h : 4 * h + 4], cols_emb[8 + 4 * h : 12 + 4 * h]], 0)
        for r in range(8):
            emb_out[2 * r + h, 0:8, :] = block
            emb_out[2 * r + h, 8:9, :] = rows_emb[r : r + 1]
            emb_out[2 * r + h, 9:10, :] = rows_emb[r + 8 : r + 9]
            emb_out[2 * r + h, 10:16, :] = jnp.zeros((6, CH), F32)
    send_all(2, lambda peer: emb_out.at[peer], emb_in)
    emb_in[pl.ds(me, 1)] = emb_out[pl.ds(me, 1)]

    tgt_rows[...] = jnp.zeros_like(tgt_rows)
    for d in range(N_SEQ):
        tgt_rows[2 * d : 2 * d + 2, :] = late_in[d, 4:6, :]
    tgt_t[...] = tgt_rows[...].T

    def chain_order(load):
        pieces = []
        for q in range(8):
            for s in range(4):
                pieces.append(load(q + 8 * s))
        return jnp.concatenate(pieces, axis=0)

    target = chain_order(lambda m: tgt_t[pl.ds(8 * m + 4 * half, 4), :])
    target = (target - 7.5) * 0.25

    wait_recv(2, emb_in)

    for d in range(N_SEQ):
        rows_scr[2 * d : 2 * d + 2, :] = emb_in[d, 8:10, :]
    cols = chain_order(lambda m: emb_in[m // 2, 4 * (m % 2) : 4 * (m % 2) + 4, :])
    zero_four = jnp.zeros((4, CH), F32)

    def put_row(ref, index, values):
        ref[index, 16:144, :] = values.astype(BF16)
        ref[index, 0:16, :] = jnp.concatenate([zero_four, values[112:124]], axis=0).astype(BF16)
        ref[index, 144:160, :] = jnp.concatenate([values[4:16], zero_four], axis=0).astype(BF16)

    def hidden_body(u, carry):
        summed = cols + rows_scr[pl.ds(u, 1), :]
        value, slope = gelu_and_slope(summed)
        slope_scr[u] = slope
        put_row(hid, u + 1, value)
        return carry

    lax.fori_loop(0, 32, hidden_body, 0, unroll=4)

    out_scale = out_w_ref[...].astype(F32)
    small_scale = out_scale * (1.0 / math.sqrt(BINS))
    chain_lane = lax.broadcasted_iota(jnp.int32, (CH, CH), 1)

    def conv_pairs(ref, weights, v, count):
        blocks = []
        for c in range(count):
            row = 2 * (v * count + c)
            blocks.append(
                jnp.concatenate(
                    [
                        ref[row + a, 16 * b : 16 * b + 128, :]
                        for a in range(4)
                        for b in range(3)
                    ],
                    axis=1,
                )
            )
        return jnp.dot(jnp.concatenate(blocks, axis=0), weights, preferred_element_type=F32)

    PAIRS = 8

    def forward_body(v, diff):
        conv = conv_pairs(hid, fwd_w[...], v, PAIRS)
        for c in range(PAIRS):
            for e in range(2):
                u = 2 * (v * PAIRS + c) + e
                out = conv[128 * c : 128 * c + 128, CH * e : CH * e + CH]
                value, slope = gelu_and_slope(out)
                summed = (hid[u + 1, 16:144, :].astype(F32) + value) * out_scale
                summed = summed - jnp.where(chain_lane == u, target, 0.0)
                error = jnp.sum(summed, axis=1, keepdims=True)
                direct = error * small_scale
                direct_scr[u] = direct
                put_row(cgrad, u + 1, direct * slope)
                diff = jnp.where(chain_lane == u, error, diff)
        return diff

    errors = lax.fori_loop(0, 16 // PAIRS, forward_body, jnp.zeros((CH, CH), F32))
    predicted = errors + target

    def backward_body(v, colsum):
        conv = conv_pairs(cgrad, bwd_w[...], v, PAIRS)
        for c in range(PAIRS):
            for e in range(2):
                u = 2 * (v * PAIRS + c) + e
                out = conv[128 * c : 128 * c + 128, CH * e : CH * e + CH]
                grad = (direct_scr[u] + out) * slope_scr[u]
                rowsum[pl.ds(u, 1), :] = jnp.sum(grad, axis=0, keepdims=True)
                colsum = colsum + grad
        return colsum

    colsum = lax.fori_loop(0, 16 // PAIRS, backward_body, jnp.zeros((CH, CH), F32))

    pred_t[...] = jnp.zeros_like(pred_t)
    for q in range(8):
        for s in range(4):
            at = 16 * q + 4 * s
            pred_t[pl.ds(8 * (q + 8 * s) + 4 * half, 4), :] = predicted[at : at + 4]
    home = pred_t[...].T
    for d in range(N_SEQ):
        for e in range(2):
            m = 2 * d + e
            at = 16 * (m % 8) + 4 * (m // 8)
            part_out[d, 4 * e : 4 * e + 4, :] = colsum[at : at + 4]
            part_out[d, 10 + e : 11 + e, :] = home[m : m + 1, 0:CH]
            part_out[d, 12 + e : 13 + e, :] = home[m : m + 1, CH : 2 * CH]
        part_out[d, 8:10, :] = rowsum[2 * d : 2 * d + 2, :]
        part_out[d, 14:16, :] = jnp.zeros((2, CH), F32)
    send_all(3, lambda peer: part_out.at[peer], part_in)
    part_in[pl.ds(me, 1)] = part_out[pl.ds(me, 1)]

    wait_recv(3, part_in)
    for r in range(8):
        both = part_in[2 * r, 10:14, :] + part_in[2 * r + 1, 10:14, :]
        for e in range(2):
            pred_ref[r + 8 * e : r + 8 * e + 1, 0:CH] = both[e : e + 1]
            pred_ref[r + 8 * e : r + 8 * e + 1, CH : 2 * CH] = both[2 + e : 3 + e]
    col_halves = []
    for h in range(2):
        total = part_in[h, 0:8, :]
        for r in range(1, 8):
            total = total + part_in[2 * r + h, 0:8, :]
        col_halves.append(total)
    col_grad = jnp.concatenate(
        [
            col_halves[0][0:4],
            col_halves[1][0:4],
            col_halves[0][4:8],
            col_halves[1][4:8],
        ],
        axis=0,
    )
    row_pairs = [part_in[2 * r, 8:10, :] + part_in[2 * r + 1, 8:10, :] for r in range(8)]
    row_grad = jnp.concatenate(
        [pair[0:1] for pair in row_pairs] + [pair[1:2] for pair in row_pairs], axis=0
    )
    grads = jnp.concatenate([row_grad, col_grad], axis=1)
    high = grads.astype(BF16)
    rest = grads - high.astype(F32)
    middle = rest.astype(BF16)
    low = (rest - middle.astype(F32)).astype(BF16)
    stacked = jnp.concatenate([high, middle, low], axis=0)
    wide = lax.dot_general(
        stacked,
        proj[...],
        (((1,), (1,)), ((), ())),
        preferred_element_type=F32,
    )
    grad_ref[...] = (wide[32:48] + wide[16:32]) + wide[0:16]

    wait_send(0, stat_in)
    wait_send(1, late_in)
    wait_send(2, emb_in)
    wait_send(3, part_in)


def deliver(pred_in, grad_in, pred_out, grad_out):
    pred_out[...] = pred_in[...]
    grad_out[...] = grad_in[...]


def per_device(
    bases, stem_weight, conv_weight, row_proj, col_proj, pair_weight, out_weight, targets
):
    vmem = pl.BlockSpec(memory_space=pltpu.VMEM)
    hbm = pl.BlockSpec(memory_space=pl.ANY)
    shapes = (
        jax.ShapeDtypeStruct((LOCAL, BINS), F32),
        jax.ShapeDtypeStruct((LOCAL, TRUNK_CH), F32),
    )
    results = pl.pallas_call(
        fused,
        out_shape=shapes,
        in_specs=[hbm] * 8,
        out_specs=(vmem, vmem),
        scratch_shapes=[
            pltpu.VMEM((ROWS, POOL), jnp.int32),
            pltpu.VMEM((20, STEM_CH), BF16),
            pltpu.VMEM((1, CH), BF16),
            pltpu.VMEM((LOCAL, BINS), jnp.int32),
            pltpu.VMEM((2, 8, POOL), jnp.int32),
            pltpu.VMEM((ROWS + 16, POOL), jnp.int32),
            pltpu.VMEM((264, POOL), jnp.int32),
            pltpu.VMEM((32, STEM_CH), F32),
            pltpu.VMEM((2, GROUP * POOL, 32), BF16),
            pltpu.VMEM((2, GROUP, STEM_CH), F32),
            pltpu.VMEM((OFF + ROWS + 16, STEM_CH), F32),
            pltpu.VMEM((ROWS, 5 * STEM_CH), BF16),
            pltpu.VMEM((TILES, 5 * STEM_CH, 256), BF16),
            pltpu.VMEM((TILES, LOCAL, 256), F32),
            pltpu.VMEM((TRUNK_CH, 2 * CH), BF16),
            pltpu.VMEM((9 * CH, CH), BF16),
            pltpu.VMEM((16, 256), F32),
            pltpu.VMEM((8, 256), F32),
            pltpu.VMEM((N_SEQ, 8, 256), F32),
            pltpu.VMEM((8, 8, 256), F32),
            pltpu.VMEM((N_SEQ, 8, 256), F32),
            pltpu.VMEM((N_SEQ, 16, CH), F32),
            pltpu.VMEM((N_SEQ, 16, CH), F32),
            pltpu.VMEM((CH, BINS), F32),
            pltpu.VMEM((BINS, CH), F32),
            pltpu.VMEM((12 * CH, 2 * CH), BF16),
            pltpu.VMEM((12 * CH, 2 * CH), BF16),
            pltpu.VMEM((32, CH), F32),
            pltpu.VMEM((34, 160, CH), BF16),
            pltpu.VMEM((32, CH, CH), F32),
            pltpu.VMEM((32, CH, CH), F32),
            pltpu.VMEM((34, 160, CH), BF16),
            pltpu.VMEM((BINS, CH), F32),
            pltpu.VMEM((32, CH), F32),
            pltpu.VMEM((N_SEQ, 16, CH), F32),
            pltpu.VMEM((N_SEQ, 16, CH), F32),
            pltpu.SemaphoreType.DMA((4,)),
            pltpu.SemaphoreType.DMA((TILES,)),
            pltpu.SemaphoreType.DMA((3,)),
            pltpu.SemaphoreType.DMA((2,)),
            pltpu.SemaphoreType.DMA((2,)),
            pltpu.SemaphoreType.DMA((4,)),
            pltpu.SemaphoreType.DMA((4,)),
        ],
        compiler_params=pltpu.CompilerParams(
            collective_id=0, has_side_effects=True, vmem_limit_bytes=56 << 20
        ),
    )(
        bases.reshape(ROWS, POOL),
        stem_weight,
        conv_weight.reshape(5 * STEM_CH, TRUNK_CH),
        row_proj,
        col_proj,
        pair_weight.reshape(9 * CH, CH),
        out_weight.reshape(1, CH),
        targets,
    )
    return pl.pallas_call(
        deliver, out_shape=shapes, in_specs=[vmem, vmem], out_specs=(vmem, vmem)
    )(*results)


def solution(mesh):
    in_specs = (P(("dp", "seq")), P(), P(), P(), P(), P(), P(), P(("dp", "seq"), None))
    out_specs = (P(("dp", "seq"), None), P(("dp", "seq"), None))
    return jax.shard_map(
        per_device, mesh=mesh, in_specs=in_specs, out_specs=out_specs, check_vma=False
    )
```

```python
import functools
import math

import jax
import jax.numpy as jnp
from jax import lax
from jax.experimental import pallas as pl
from jax.experimental.pallas import tpu as pltpu
from jax.sharding import PartitionSpec as P

MESH = pl.DeviceIdType.MESH
FAR_FIRST = sorted(
    [(z, x, c) for z in range(2) for x in range(4) for c in range(2) if (z, x, c) != (0, 0, 0)],
    key=lambda d: -(d[0] + min(d[1], 4 - d[1]) + 0.1 * d[2]),
)
F32 = jnp.float32
BF16 = jnp.bfloat16

N_SEQ = 16
STEM_CH = 768
TRUNK_CH = 1536
CH = 128
POOL = 128
ROWS = 256
BINS = 256
LOCAL = 16
GROUP = 24
TILES = TRUNK_CH // 256
C0 = math.sqrt(2.0 / math.pi)


def gelu(x):
    half = 0.5 * x
    return half + half * jnp.tanh(x * (C0 + (C0 * 0.044715) * (x * x)))


def gelu_and_slope(x):
    square = x * x
    a = 0.5 + 0.5 * jnp.tanh(x * (C0 + (C0 * 0.044715) * square))
    value = x * a
    slope = a + value * (1.0 - a) * (2.0 * C0 + (6.0 * C0 * 0.044715) * square)
    return value, slope


def fused(
    bases_hbm,
    stem_hbm,
    conv_ref,
    row_proj_ref,
    col_proj_ref,
    pair_hbm,
    out_w_hbm,
    targets_hbm,
    pred_ref,
    grad_ref,
    bases_ref,
    stem_ref,
    out_w_ref,
    targets_ref,
    halo,
    ext,
    codes_in_order,
    codes,
    stem_w,
    onehot,
    extremes,
    pooled1,
    taps,
    conv_w,
    pooled2,
    proj,
    pair_ref,
    stat_all,
    stat_out,
    stat_in,
    late_out,
    late_in,
    emb_out,
    emb_in,
    tgt_rows,
    tgt_t,
    fwd_w,
    bwd_w,
    rows_scr,
    hid,
    slope_scr,
    direct_scr,
    cgrad,
    pred_t,
    rowsum,
    part_out,
    part_in,
    input_sems,
    conv_sems,
    weight_sems,
    halo_send,
    halo_recv,
    send_sems,
    recv_sems,
):
    me = lax.axis_index("seq")
    rho = me // 2
    half = me % 2
    z, x, core = me // 8, lax.rem(me // 2, 4), half
    first = me == 0
    last = me == N_SEQ - 1

    input_copies = [
        pltpu.make_async_copy(bases_hbm, bases_ref, input_sems.at[0]),
        pltpu.make_async_copy(stem_hbm, stem_ref, input_sems.at[1]),
        pltpu.make_async_copy(out_w_hbm, out_w_ref, input_sems.at[2]),
        pltpu.make_async_copy(targets_hbm, targets_ref, input_sems.at[3]),
    ]
    for copy in input_copies:
        copy.start()
    conv_copies = [
        pltpu.make_async_copy(
            conv_ref.at[:, pl.ds(256 * q, 256)], conv_w.at[q], conv_sems.at[q]
        )
        for q in range(TILES)
    ]
    weight_copies = [
        pltpu.make_async_copy(row_proj_ref, proj.at[:, pl.ds(0, CH)], weight_sems.at[0]),
        pltpu.make_async_copy(col_proj_ref, proj.at[:, pl.ds(CH, CH)], weight_sems.at[1]),
        pltpu.make_async_copy(pair_hbm, pair_ref, weight_sems.at[2]),
    ]

    barrier = pltpu.get_barrier_semaphore()

    def greet(k, carry):
        peer = lax.rem(me + k, N_SEQ)
        pl.semaphore_signal(barrier, inc=1, device_id={"seq": peer}, device_id_type=MESH)
        return carry

    lax.fori_loop(1, N_SEQ, greet, 0)

    ext[...] = jnp.zeros_like(ext)
    for copy in input_copies:
        copy.wait()
    ext[8 : 8 + ROWS, :] = bases_ref[...] + 1
    stem_w[...] = jnp.zeros_like(stem_w)
    stem_w[0:20, :] = stem_ref[...].astype(F32)

    def send_all(index, source_of, landing):
        for dz, dx, dc in FAR_FIRST:
            peer = 8 * lax.rem(z + dz, 2) + 2 * lax.rem(x + dx, 4) + lax.rem(core + dc, 2)
            pltpu.make_async_remote_copy(
                src_ref=source_of(peer),
                dst_ref=landing.at[me],
                send_sem=send_sems.at[index],
                recv_sem=recv_sems.at[index],
                device_id={"seq": peer},
                device_id_type=MESH,
            ).start()

    def wait_recv(index, landing):
        blocks = landing.at[pl.ds(0, N_SEQ - 1)]
        pltpu.make_async_copy(blocks, blocks, recv_sems.at[index]).wait()

    def wait_send(index, landing):
        blocks = landing.at[pl.ds(0, N_SEQ - 1)]
        pltpu.make_async_copy(blocks, blocks, send_sems.at[index]).wait()

    lane = lax.broadcasted_iota(jnp.int32, (1, POOL), 1)

    def code_rows(start, count):
        total = ext[start : start + count, :] << 6
        here = ext[start : start + count, :]
        above = ext[start - 1 : start - 1 + count, :]
        below = ext[start + 1 : start + 1 + count, :]
        for shift in (1, 2):
            before = jnp.where(
                lane >= shift, pltpu.roll(here, shift, 1), pltpu.roll(above, shift, 1)
            )
            after = jnp.where(
                lane < POOL - shift,
                pltpu.roll(here, POOL - shift, 1),
                pltpu.roll(below, POOL - shift, 1),
            )
            total = total + (before << (3 * (2 - shift))) + (after << (3 * (2 + shift)))
        return total

    codes_in_order[...] = code_rows(8, ROWS)
    for q in range(1, 15):
        codes[16 * (q - 1) : 16 * q, :] = codes_in_order[pl.ds(q, 16, stride=16), :]

    sub = lax.broadcasted_iota(jnp.int32, (8, POOL), 0)
    base_code = (sub & 3) + 1
    tap_shift = (sub >> 2) * 3
    zero_rows = jnp.zeros((8, POOL), F32)

    def onehot_rows(start, r):
        code = jnp.broadcast_to(codes[pl.ds(start + r, 1), :], (8, POOL))
        pairs = [
            jnp.where(((code >> (tap_shift + 6 * k)) & 7) == base_code, 1.0, 0.0).astype(F32)
            for k in range(3)
        ]
        return jnp.concatenate(pairs + [zero_rows], axis=0).astype(BF16).T

    def pooled_rows():
        values = jnp.maximum(gelu(extremes[0]), gelu(extremes[1]))
        return values.astype(BF16).astype(F32)

    up = pltpu.make_async_remote_copy(
        src_ref=bases_ref.at[pl.ds(ROWS - 8, 8)],
        dst_ref=halo.at[0],
        send_sem=halo_send.at[0],
        recv_sem=halo_recv.at[0],
        device_id={"seq": lax.rem(me + 1, N_SEQ)},
        device_id_type=MESH,
    )
    down = pltpu.make_async_remote_copy(
        src_ref=bases_ref.at[pl.ds(0, 8)],
        dst_ref=halo.at[1],
        send_sem=halo_send.at[1],
        recv_sem=halo_recv.at[1],
        device_id={"seq": lax.rem(me + N_SEQ - 1, N_SEQ)},
        device_id_type=MESH,
    )

    def first_onehot(r, carry):
        onehot[0, pl.ds(pl.multiple_of(POOL * r, POOL), POOL), :] = onehot_rows(0, r)
        return carry

    lax.fori_loop(0, GROUP, first_onehot, 0, unroll=12)
    extremes[...] = jnp.zeros_like(extremes)

    def stem_body(g, carry):
        @pl.when(g == 2)
        def _():
            pl.semaphore_wait(barrier, N_SEQ - 1)
            up.start()
            down.start()
            for copy in conv_copies + weight_copies:
                copy.start()

        @pl.when(g == 8)
        def _():
            up.wait()
            down.wait()
            ext[0:8, :] = jnp.where(first, 0, halo[0] + 1)
            ext[8 + ROWS : 16 + ROWS, :] = jnp.where(last, 0, halo[1] + 1)
            begin = code_rows(6, 3)
            end = code_rows(7 + ROWS, 3)
            codes_in_order[0:1, :] = begin[2:3]
            codes_in_order[ROWS - 1 : ROWS, :] = end[0:1]
            codes[224:240, :] = codes_in_order[pl.ds(0, 16, stride=16), :]
            codes[240:256, :] = codes_in_order[pl.ds(15, 16, stride=16), :]
            codes[256:258, :] = begin[0:2]
            codes[258:260, :] = end[1:3]
            codes[260:264, :] = jnp.zeros((4, POOL), jnp.int32)

        @pl.when(g == 10)
        def _():
            for copy in conv_copies:
                copy.wait()

        slot = lax.rem(g, 2)
        pooled1[pl.ds(pl.multiple_of(g * GROUP, 8), GROUP), :] = pooled_rows()
        for n in range(STEM_CH // 256):
            stem = jnp.dot(
                onehot[slot],
                stem_w[:, 256 * n : 256 * n + 256].astype(BF16),
                preferred_element_type=F32,
            ).reshape(GROUP, POOL, 256)
            extremes[0, :, 256 * n : 256 * n + 256] = jnp.max(stem, axis=1)
            extremes[1, :, 256 * n : 256 * n + 256] = jnp.min(stem, axis=1)
        start = pl.multiple_of(jnp.minimum(g + 1, 10) * GROUP, 8)
        for r in range(GROUP):
            onehot[1 - slot, POOL * r : POOL * r + POOL, :] = onehot_rows(start, r)
        return carry

    lax.fori_loop(0, 11, stem_body, 0)
    pooled1[11 * GROUP : 12 * GROUP, :] = pooled_rows()

    for r in range(8):
        for e in range(2):
            late_out[r, 4 + e : 5 + e, :] = targets_ref[r + 8 * e : r + 8 * e + 1, :].astype(F32)
        late_out[r, 6:8, :] = jnp.zeros((2, 256), F32)

    def stem_tile(q):
        at = GROUP + (16 * (q - 1) if 1 <= q <= 14 else 224 + (q // 15) * 16)
        return pooled1[at : at + 16, :]

    outer = pooled1[GROUP + 256 : GROUP + 264, :]
    before = jnp.where(first, 0.0, outer[0:2])
    after = jnp.where(last, 0.0, outer[2:4])
    for q in range(16):
        taps[16 * (q + 2) : 16 * (q + 3), :] = stem_tile(q).astype(BF16)
    for e in range(2):
        taps[16 * e : 16 * e + 16, :] = jnp.concatenate(
            [before[e : e + 1], stem_tile(14 + e)[0:15]], axis=0
        ).astype(BF16)
        taps[16 * (18 + e) : 16 * (19 + e), :] = jnp.concatenate(
            [stem_tile(e)[1:16], after[e : e + 1]], axis=0
        ).astype(BF16)

    def trunk_tile(q):
        windows = [taps[16 * k : 16 * k + ROWS, :] for k in range(5)]
        trunk = jnp.dot(
            jnp.concatenate(windows, axis=1), conv_w[q], preferred_element_type=F32
        ).reshape(16, LOCAL, 256)
        block = jnp.maximum(gelu(jnp.max(trunk, axis=0)), gelu(jnp.min(trunk, axis=0)))
        pooled2[q] = block
        total = jnp.sum(block, axis=0, keepdims=True)
        return total, jnp.sum(block * block, axis=0, keepdims=True)

    for q in range(TILES):
        total, square = trunk_tile(q)
        stat_all[q : q + 1, :] = total
        stat_all[8 + q : 9 + q, :] = square
        if q == 3:
            stat_out[0:4, :] = stat_all[0:4, :]
            stat_out[4:8, :] = stat_all[8:12, :]
            send_all(0, lambda peer: stat_out, stat_in)
    stat_in[pl.ds(me, 1)] = stat_out[...][None]
    for r in range(8):
        late_out[r, 0:2, :] = stat_all[4:6, :]
        late_out[r, 2:4, :] = stat_all[12:14, :]
    send_all(1, lambda peer: late_out.at[peer // 2], late_in)
    late_in[pl.ds(me, 1)] = late_out[pl.ds(rho, 1)]

    for copy in weight_copies:
        copy.wait()
    zero_block = jnp.zeros((CH, CH), BF16)
    for a in range(4):
        for b in range(3):
            at = (3 * a + b) * CH
            near = pair_ref[(3 * a + b) * CH : (3 * a + b + 1) * CH, :] if a < 3 else zero_block
            far = (
                pair_ref[(3 * (a - 1) + b) * CH : (3 * (a - 1) + b + 1) * CH, :]
                if a > 0
                else zero_block
            )
            fwd_w[at : at + CH, :] = jnp.concatenate([near, far], axis=1)
            near = (
                pair_ref[(3 * (2 - a) + 2 - b) * CH : (3 * (2 - a) + 3 - b) * CH, :].T
                if a < 3
                else zero_block
            )
            far = (
                pair_ref[(3 * (3 - a) + 2 - b) * CH : (3 * (3 - a) + 3 - b) * CH, :].T
                if a > 0
                else zero_block
            )
            bwd_w[at : at + CH, :] = jnp.concatenate([near, far], axis=1)

    zero_row = jnp.zeros((160, CH), BF16)
    hid[0] = zero_row
    hid[33] = zero_row
    cgrad[0] = zero_row
    cgrad[33] = zero_row

    wait_recv(0, stat_in)
    early = jnp.sum(stat_in[...], axis=0)
    wait_recv(1, late_in)
    late = jnp.sum(late_in[...], axis=0)
    mean = jnp.concatenate([early[0:4], late[0:2]], axis=0) / BINS
    var = jnp.concatenate([early[4:8], late[2:4]], axis=0) / BINS - mean * mean
    scale = lax.rsqrt(var + 1e-05)
    normed = jnp.concatenate(
        [
            ((pooled2[q] - mean[q : q + 1]) * scale[q : q + 1]).astype(BF16)
            for q in range(TILES)
        ],
        axis=1,
    )
    emb = jnp.dot(normed, proj[...], preferred_element_type=F32)
    rows_emb = emb[:, 0:CH]
    cols_emb = emb[:, CH : 2 * CH]
    zero_six = jnp.zeros((6, CH), F32)
    for h in range(2):
        block = [cols_emb[4 * h : 4 * h + 4], cols_emb[8 + 4 * h : 12 + 4 * h]]
        for r in range(8):
            pair = [rows_emb[r : r + 1], rows_emb[r + 8 : r + 9]]
            emb_out[2 * r + h] = jnp.concatenate(block + pair + [zero_six], 0).astype(BF16)
    send_all(2, lambda peer: emb_out.at[peer], emb_in)
    emb_in[pl.ds(me, 1)] = emb_out[pl.ds(me, 1)]

    tgt_rows[...] = jnp.zeros_like(tgt_rows)
    for d in range(N_SEQ):
        tgt_rows[2 * d : 2 * d + 2, :] = late_in[d, 4:6, :]
    tgt_t[...] = tgt_rows[...].T

    def chain_order(load):
        pieces = []
        for q in range(8):
            for s in range(4):
                pieces.append(load(q + 8 * s))
        return jnp.concatenate(pieces, axis=0)

    target = chain_order(lambda m: tgt_t[pl.ds(8 * m + 4 * half, 4), :])
    target = (target - 7.5) * 0.25

    wait_recv(2, emb_in)

    embs = [emb_in[d].astype(F32) for d in range(N_SEQ)]
    for d in range(N_SEQ):
        rows_scr[2 * d : 2 * d + 2, :] = embs[d][8:10]
    cols = chain_order(lambda m: embs[m // 2][4 * (m % 2) : 4 * (m % 2) + 4])
    zero_four = jnp.zeros((4, CH), F32)

    def put_row(ref, index, values):
        ref[index, 16:144, :] = values.astype(BF16)
        ref[index, 0:16, :] = jnp.concatenate([zero_four, values[112:124]], axis=0).astype(BF16)
        ref[index, 144:160, :] = jnp.concatenate([values[4:16], zero_four], axis=0).astype(BF16)

    def hidden_body(u, carry):
        summed = cols + rows_scr[pl.ds(u, 1), :]
        value, slope = gelu_and_slope(summed)
        slope_scr[u] = slope
        put_row(hid, u + 1, value)
        return carry

    lax.fori_loop(0, 32, hidden_body, 0, unroll=4)

    out_scale = out_w_ref[...].astype(F32)
    small_scale = out_scale * (1.0 / math.sqrt(BINS))
    chain_lane = lax.broadcasted_iota(jnp.int32, (CH, CH), 1)

    def conv_pairs(ref, weights, v, count):
        blocks = []
        for c in range(count):
            row = 2 * (v * count + c)
            blocks.append(
                jnp.concatenate(
                    [
                        ref[row + a, 16 * b : 16 * b + 128, :]
                        for a in range(4)
                        for b in range(3)
                    ],
                    axis=1,
                )
            )
        return jnp.dot(jnp.concatenate(blocks, axis=0), weights, preferred_element_type=F32)

    PAIRS = 8

    def forward_body(v, diff):
        conv = conv_pairs(hid, fwd_w[...], v, PAIRS)
        for c in range(PAIRS):
            for e in range(2):
                u = 2 * (v * PAIRS + c) + e
                out = conv[128 * c : 128 * c + 128, CH * e : CH * e + CH]
                value, slope = gelu_and_slope(out)
                summed = (hid[u + 1, 16:144, :].astype(F32) + value) * out_scale
                summed = summed - jnp.where(chain_lane == u, target, 0.0)
                error = jnp.sum(summed, axis=1, keepdims=True)
                direct = error * small_scale
                direct_scr[u] = direct
                put_row(cgrad, u + 1, direct * slope)
                diff = jnp.where(chain_lane == u, error, diff)
        return diff

    errors = lax.fori_loop(0, 16 // PAIRS, forward_body, jnp.zeros((CH, CH), F32))
    predicted = errors + target

    def backward_body(v, colsum):
        conv = conv_pairs(cgrad, bwd_w[...], v, PAIRS)
        for c in range(PAIRS):
            for e in range(2):
                u = 2 * (v * PAIRS + c) + e
                out = conv[128 * c : 128 * c + 128, CH * e : CH * e + CH]
                grad = (direct_scr[u] + out) * slope_scr[u]
                rowsum[pl.ds(u, 1), :] = jnp.sum(grad, axis=0, keepdims=True)
                colsum = colsum + grad
        return colsum

    colsum = lax.fori_loop(0, 16 // PAIRS, backward_body, jnp.zeros((CH, CH), F32))

    pred_t[...] = jnp.zeros_like(pred_t)
    for q in range(8):
        for s in range(4):
            at = 16 * q + 4 * s
            pred_t[pl.ds(8 * (q + 8 * s) + 4 * half, 4), :] = predicted[at : at + 4]
    home = pred_t[...].T
    for d in range(N_SEQ):
        for e in range(2):
            m = 2 * d + e
            at = 16 * (m % 8) + 4 * (m // 8)
            part_out[d, 4 * e : 4 * e + 4, :] = colsum[at : at + 4]
            part_out[d, 10 + e : 11 + e, :] = home[m : m + 1, 0:CH]
            part_out[d, 12 + e : 13 + e, :] = home[m : m + 1, CH : 2 * CH]
        part_out[d, 8:10, :] = rowsum[2 * d : 2 * d + 2, :]
        part_out[d, 14:16, :] = jnp.zeros((2, CH), F32)
    send_all(3, lambda peer: part_out.at[peer], part_in)
    part_in[pl.ds(me, 1)] = part_out[pl.ds(me, 1)]

    wait_recv(3, part_in)
    for r in range(8):
        both = part_in[2 * r, 10:14, :] + part_in[2 * r + 1, 10:14, :]
        for e in range(2):
            pred_ref[r + 8 * e : r + 8 * e + 1, 0:CH] = both[e : e + 1]
            pred_ref[r + 8 * e : r + 8 * e + 1, CH : 2 * CH] = both[2 + e : 3 + e]
    col_halves = []
    for h in range(2):
        total = part_in[h, 0:8, :]
        for r in range(1, 8):
            total = total + part_in[2 * r + h, 0:8, :]
        col_halves.append(total)
    col_grad = jnp.concatenate(
        [
            col_halves[0][0:4],
            col_halves[1][0:4],
            col_halves[0][4:8],
            col_halves[1][4:8],
        ],
        axis=0,
    )
    row_pairs = [part_in[2 * r, 8:10, :] + part_in[2 * r + 1, 8:10, :] for r in range(8)]
    row_grad = jnp.concatenate(
        [pair[0:1] for pair in row_pairs] + [pair[1:2] for pair in row_pairs], axis=0
    )
    grads = jnp.concatenate([row_grad, col_grad], axis=1)
    high = grads.astype(BF16)
    rest = grads - high.astype(F32)
    middle = rest.astype(BF16)
    low = (rest - middle.astype(F32)).astype(BF16)
    stacked = jnp.concatenate([high, middle, low], axis=0)
    wide = lax.dot_general(
        stacked,
        proj[...],
        (((1,), (1,)), ((), ())),
        preferred_element_type=F32,
    )
    grad_ref[...] = (wide[32:48] + wide[16:32]) + wide[0:16]

    wait_send(0, stat_in)
    wait_send(1, late_in)
    wait_send(2, emb_in)
    wait_send(3, part_in)


def deliver(pred_in, grad_in, pred_out, grad_out):
    pred_out[...] = pred_in[...]
    grad_out[...] = grad_in[...]


def per_device(
    bases, stem_weight, conv_weight, row_proj, col_proj, pair_weight, out_weight, targets
):
    vmem = pl.BlockSpec(memory_space=pltpu.VMEM)
    hbm = pl.BlockSpec(memory_space=pl.ANY)
    shapes = (
        jax.ShapeDtypeStruct((LOCAL, BINS), F32),
        jax.ShapeDtypeStruct((LOCAL, TRUNK_CH), F32),
    )
    results = pl.pallas_call(
        fused,
        out_shape=shapes,
        in_specs=[hbm] * 8,
        out_specs=(vmem, vmem),
        scratch_shapes=[
            pltpu.VMEM((ROWS, POOL), jnp.int32),
            pltpu.VMEM((20, STEM_CH), BF16),
            pltpu.VMEM((1, CH), BF16),
            pltpu.VMEM((LOCAL, BINS), jnp.int32),
            pltpu.VMEM((2, 8, POOL), jnp.int32),
            pltpu.VMEM((ROWS + 16, POOL), jnp.int32),
            pltpu.VMEM((ROWS, POOL), jnp.int32),
            pltpu.VMEM((264, POOL), jnp.int32),
            pltpu.VMEM((32, STEM_CH), F32),
            pltpu.VMEM((2, GROUP * POOL, 32), BF16),
            pltpu.VMEM((2, GROUP, STEM_CH), F32),
            pltpu.VMEM((12 * GROUP, STEM_CH), F32),
            pltpu.VMEM((20 * 16, STEM_CH), BF16),
            pltpu.VMEM((TILES, 5 * STEM_CH, 256), BF16),
            pltpu.VMEM((TILES, LOCAL, 256), F32),
            pltpu.VMEM((TRUNK_CH, 2 * CH), BF16),
            pltpu.VMEM((9 * CH, CH), BF16),
            pltpu.VMEM((16, 256), F32),
            pltpu.VMEM((8, 256), F32),
            pltpu.VMEM((N_SEQ, 8, 256), F32),
            pltpu.VMEM((8, 8, 256), F32),
            pltpu.VMEM((N_SEQ, 8, 256), F32),
            pltpu.VMEM((N_SEQ, 16, CH), BF16),
            pltpu.VMEM((N_SEQ, 16, CH), BF16),
            pltpu.VMEM((CH, BINS), F32),
            pltpu.VMEM((BINS, CH), F32),
            pltpu.VMEM((12 * CH, 2 * CH), BF16),
            pltpu.VMEM((12 * CH, 2 * CH), BF16),
            pltpu.VMEM((32, CH), F32),
            pltpu.VMEM((34, 160, CH), BF16),
            pltpu.VMEM((32, CH, CH), F32),
            pltpu.VMEM((32, CH, CH), F32),
            pltpu.VMEM((34, 160, CH), BF16),
            pltpu.VMEM((BINS, CH), F32),
            pltpu.VMEM((32, CH), F32),
            pltpu.VMEM((N_SEQ, 16, CH), F32),
            pltpu.VMEM((N_SEQ, 16, CH), F32),
            pltpu.SemaphoreType.DMA((4,)),
            pltpu.SemaphoreType.DMA((TILES,)),
            pltpu.SemaphoreType.DMA((3,)),
            pltpu.SemaphoreType.DMA((2,)),
            pltpu.SemaphoreType.DMA((2,)),
            pltpu.SemaphoreType.DMA((4,)),
            pltpu.SemaphoreType.DMA((4,)),
        ],
        compiler_params=pltpu.CompilerParams(
            collective_id=0, has_side_effects=True, vmem_limit_bytes=56 << 20
        ),
    )(
        bases.reshape(ROWS, POOL),
        stem_weight,
        conv_weight.reshape(5 * STEM_CH, TRUNK_CH),
        row_proj,
        col_proj,
        pair_weight.reshape(9 * CH, CH),
        out_weight.reshape(1, CH),
        targets,
    )
    return pl.pallas_call(
        deliver, out_shape=shapes, in_specs=[vmem, vmem], out_specs=(vmem, vmem)
    )(*results)


def solution(mesh):
    in_specs = (P(("dp", "seq")), P(), P(), P(), P(), P(), P(), P(("dp", "seq"), None))
    out_specs = (P(("dp", "seq"), None), P(("dp", "seq"), None))
    return jax.shard_map(
        per_device, mesh=mesh, in_specs=in_specs, out_specs=out_specs, check_vma=False
    )
```

```python
import functools
import math

import jax
import jax.numpy as jnp
from jax import lax
from jax.experimental import pallas as pl
from jax.experimental.pallas import tpu as pltpu
from jax.sharding import PartitionSpec as P

MESH = pl.DeviceIdType.MESH
FAR_FIRST = sorted(
    [(z, x, c) for z in range(2) for x in range(4) for c in range(2) if (z, x, c) != (0, 0, 0)],
    key=lambda d: -(d[0] + min(d[1], 4 - d[1]) + 0.1 * d[2]),
)
F32 = jnp.float32
BF16 = jnp.bfloat16

N_SEQ = 16
STEM_CH = 768
TRUNK_CH = 1536
CH = 128
POOL = 128
ROWS = 256
BINS = 256
LOCAL = 16
GROUP = 24
TILES = TRUNK_CH // 256
C0 = math.sqrt(2.0 / math.pi)


def gelu(x):
    half = 0.5 * x
    return half + half * jnp.tanh(x * (C0 + (C0 * 0.044715) * (x * x)))


def gelu_and_slope(x):
    square = x * x
    a = 0.5 + 0.5 * jnp.tanh(x * (C0 + (C0 * 0.044715) * square))
    value = x * a
    slope = a + value * (1.0 - a) * (2.0 * C0 + (6.0 * C0 * 0.044715) * square)
    return value, slope


def fused(
    bases_hbm,
    stem_hbm,
    conv_ref,
    row_proj_ref,
    col_proj_ref,
    pair_hbm,
    out_w_hbm,
    targets_hbm,
    pred_ref,
    grad_ref,
    bases_ref,
    stem_ref,
    out_w_ref,
    targets_ref,
    halo,
    ext,
    codes_in_order,
    codes,
    stem_w,
    onehot,
    extremes,
    pooled1,
    taps,
    conv_w,
    pooled2,
    proj,
    pair_ref,
    stat_all,
    stat_out,
    stat_in,
    late_out,
    late_in,
    emb_out,
    emb_in,
    tgt_rows,
    tgt_t,
    fwd_w,
    bwd_w,
    rows_scr,
    hid,
    slope_scr,
    direct_scr,
    cgrad,
    pred_t,
    rowsum,
    part_out,
    part_in,
    input_sems,
    conv_sems,
    weight_sems,
    halo_send,
    halo_recv,
    send_sems,
    recv_sems,
):
    me = lax.axis_index("seq")
    rho = me // 2
    half = me % 2
    z, x, core = me // 8, lax.rem(me // 2, 4), half
    first = me == 0
    last = me == N_SEQ - 1

    input_copies = [
        pltpu.make_async_copy(bases_hbm, bases_ref, input_sems.at[0]),
        pltpu.make_async_copy(stem_hbm, stem_ref, input_sems.at[1]),
        pltpu.make_async_copy(out_w_hbm, out_w_ref, input_sems.at[2]),
        pltpu.make_async_copy(targets_hbm, targets_ref, input_sems.at[3]),
    ]
    for copy in input_copies:
        copy.start()
    conv_copies = [
        pltpu.make_async_copy(
            conv_ref.at[:, pl.ds(256 * q, 256)], conv_w.at[q], conv_sems.at[q]
        )
        for q in range(TILES)
    ]
    weight_copies = [
        pltpu.make_async_copy(row_proj_ref, proj.at[:, pl.ds(0, CH)], weight_sems.at[0]),
        pltpu.make_async_copy(col_proj_ref, proj.at[:, pl.ds(CH, CH)], weight_sems.at[1]),
        pltpu.make_async_copy(pair_hbm, pair_ref, weight_sems.at[2]),
    ]

    barrier = pltpu.get_barrier_semaphore()

    def greet(k, carry):
        peer = lax.rem(me + k, N_SEQ)
        pl.semaphore_signal(barrier, inc=1, device_id={"seq": peer}, device_id_type=MESH)
        return carry

    lax.fori_loop(1, N_SEQ, greet, 0)

    ext[...] = jnp.zeros_like(ext)
    for copy in input_copies:
        copy.wait()
    ext[8 : 8 + ROWS, :] = bases_ref[...] + 1
    stem_w[...] = jnp.zeros_like(stem_w)
    stem_w[0:20, :] = stem_ref[...].astype(F32)

    def send_all(index, source_of, landing):
        for dz, dx, dc in FAR_FIRST:
            peer = 8 * lax.rem(z + dz, 2) + 2 * lax.rem(x + dx, 4) + lax.rem(core + dc, 2)
            pltpu.make_async_remote_copy(
                src_ref=source_of(peer),
                dst_ref=landing.at[me],
                send_sem=send_sems.at[index],
                recv_sem=recv_sems.at[index],
                device_id={"seq": peer},
                device_id_type=MESH,
            ).start()

    def wait_recv(index, landing):
        blocks = landing.at[pl.ds(0, N_SEQ - 1)]
        pltpu.make_async_copy(blocks, blocks, recv_sems.at[index]).wait()

    def wait_send(index, landing):
        blocks = landing.at[pl.ds(0, N_SEQ - 1)]
        pltpu.make_async_copy(blocks, blocks, send_sems.at[index]).wait()

    lane = lax.broadcasted_iota(jnp.int32, (1, POOL), 1)

    def code_rows(start, count):
        total = ext[start : start + count, :] << 6
        here = ext[start : start + count, :]
        above = ext[start - 1 : start - 1 + count, :]
        below = ext[start + 1 : start + 1 + count, :]
        for shift in (1, 2):
            before = jnp.where(
                lane >= shift, pltpu.roll(here, shift, 1), pltpu.roll(above, shift, 1)
            )
            after = jnp.where(
                lane < POOL - shift,
                pltpu.roll(here, POOL - shift, 1),
                pltpu.roll(below, POOL - shift, 1),
            )
            total = total + (before << (3 * (2 - shift))) + (after << (3 * (2 + shift)))
        return total

    codes_in_order[...] = code_rows(8, ROWS)
    for q in range(1, 15):
        codes[16 * (q - 1) : 16 * q, :] = codes_in_order[pl.ds(q, 16, stride=16), :]

    sub = lax.broadcasted_iota(jnp.int32, (8, POOL), 0)
    base_code = (sub & 3) + 1
    tap_shift = (sub >> 2) * 3
    zero_rows = jnp.zeros((8, POOL), F32)

    def onehot_rows(start, r):
        code = jnp.broadcast_to(codes[pl.ds(start + r, 1), :], (8, POOL))
        pairs = [
            jnp.where(((code >> (tap_shift + 6 * k)) & 7) == base_code, 1.0, 0.0).astype(F32)
            for k in range(3)
        ]
        return jnp.concatenate(pairs + [zero_rows], axis=0).astype(BF16).T

    def pooled_rows():
        values = jnp.maximum(gelu(extremes[0]), gelu(extremes[1]))
        return values.astype(BF16).astype(F32)

    up = pltpu.make_async_remote_copy(
        src_ref=bases_ref.at[pl.ds(ROWS - 8, 8)],
        dst_ref=halo.at[0],
        send_sem=halo_send.at[0],
        recv_sem=halo_recv.at[0],
        device_id={"seq": lax.rem(me + 1, N_SEQ)},
        device_id_type=MESH,
    )
    down = pltpu.make_async_remote_copy(
        src_ref=bases_ref.at[pl.ds(0, 8)],
        dst_ref=halo.at[1],
        send_sem=halo_send.at[1],
        recv_sem=halo_recv.at[1],
        device_id={"seq": lax.rem(me + N_SEQ - 1, N_SEQ)},
        device_id_type=MESH,
    )

    def first_onehot(r, carry):
        onehot[0, pl.ds(pl.multiple_of(POOL * r, POOL), POOL), :] = onehot_rows(0, r)
        return carry

    lax.fori_loop(0, GROUP, first_onehot, 0, unroll=12)
    extremes[...] = jnp.zeros_like(extremes)

    def stem_body(g, carry):
        @pl.when(g == 2)
        def _():
            pl.semaphore_wait(barrier, N_SEQ - 1)
            up.start()
            down.start()
            for copy in conv_copies + weight_copies:
                copy.start()

        @pl.when(g == 8)
        def _():
            up.wait()
            down.wait()
            ext[0:8, :] = jnp.where(first, 0, halo[0] + 1)
            ext[8 + ROWS : 16 + ROWS, :] = jnp.where(last, 0, halo[1] + 1)
            begin = code_rows(6, 3)
            end = code_rows(7 + ROWS, 3)
            codes_in_order[0:1, :] = begin[2:3]
            codes_in_order[ROWS - 1 : ROWS, :] = end[0:1]
            codes[224:240, :] = codes_in_order[pl.ds(0, 16, stride=16), :]
            codes[240:256, :] = codes_in_order[pl.ds(15, 16, stride=16), :]
            codes[256:258, :] = begin[0:2]
            codes[258:260, :] = end[1:3]
            codes[260:264, :] = jnp.zeros((4, POOL), jnp.int32)

        @pl.when(g == 10)
        def _():
            for copy in conv_copies:
                copy.wait()

        slot = lax.rem(g, 2)
        pooled1[pl.ds(pl.multiple_of(g * GROUP, 8), GROUP), :] = pooled_rows()
        for n in range(STEM_CH // 256):
            stem = jnp.dot(
                onehot[slot],
                stem_w[:, 256 * n : 256 * n + 256].astype(BF16),
                preferred_element_type=F32,
            ).reshape(GROUP, POOL, 256)
            extremes[0, :, 256 * n : 256 * n + 256] = jnp.max(stem, axis=1)
            extremes[1, :, 256 * n : 256 * n + 256] = jnp.min(stem, axis=1)
        start = pl.multiple_of(jnp.minimum(g + 1, 10) * GROUP, 8)
        for r in range(GROUP):
            onehot[1 - slot, POOL * r : POOL * r + POOL, :] = onehot_rows(start, r)
        return carry

    lax.fori_loop(0, 11, stem_body, 0)
    pooled1[11 * GROUP : 12 * GROUP, :] = pooled_rows()

    for r in range(8):
        for e in range(2):
            late_out[r, 4 + e : 5 + e, :] = targets_ref[r + 8 * e : r + 8 * e + 1, :].astype(F32)
        late_out[r, 6:8, :] = jnp.zeros((2, 256), F32)

    def stem_tile(q):
        at = GROUP + (16 * (q - 1) if 1 <= q <= 14 else 224 + (q // 15) * 16)
        return pooled1[at : at + 16, :]

    outer = pooled1[GROUP + 256 : GROUP + 264, :]
    before = jnp.where(first, 0.0, outer[0:2])
    after = jnp.where(last, 0.0, outer[2:4])
    for q in range(16):
        taps[16 * (q + 2) : 16 * (q + 3), :] = stem_tile(q).astype(BF16)
    for e in range(2):
        taps[16 * e : 16 * e + 16, :] = jnp.concatenate(
            [before[e : e + 1], stem_tile(14 + e)[0:15]], axis=0
        ).astype(BF16)
        taps[16 * (18 + e) : 16 * (19 + e), :] = jnp.concatenate(
            [stem_tile(e)[1:16], after[e : e + 1]], axis=0
        ).astype(BF16)

    def trunk_tile(q):
        windows = [taps[16 * k : 16 * k + ROWS, :] for k in range(5)]
        trunk = jnp.dot(
            jnp.concatenate(windows, axis=1), conv_w[q], preferred_element_type=F32
        ).reshape(16, LOCAL, 256)
        block = jnp.maximum(gelu(jnp.max(trunk, axis=0)), gelu(jnp.min(trunk, axis=0)))
        pooled2[q] = block
        total = jnp.sum(block, axis=0, keepdims=True)
        return total, jnp.sum(block * block, axis=0, keepdims=True)

    for q in range(TILES):
        total, square = trunk_tile(q)
        stat_all[q : q + 1, :] = total
        stat_all[8 + q : 9 + q, :] = square
        if q == 3:
            stat_out[0:4, :] = stat_all[0:4, :]
            stat_out[4:8, :] = stat_all[8:12, :]
            send_all(0, lambda peer: stat_out, stat_in)
    stat_in[pl.ds(me, 1)] = stat_out[...][None]
    for r in range(8):
        late_out[r, 0:2, :] = stat_all[4:6, :]
        late_out[r, 2:4, :] = stat_all[12:14, :]
    send_all(1, lambda peer: late_out.at[peer // 2], late_in)
    late_in[pl.ds(me, 1)] = late_out[pl.ds(rho, 1)]

    for copy in weight_copies:
        copy.wait()
    zero_block = jnp.zeros((CH, CH), BF16)

    def place_weights(ref, block):
        for b in range(3):
            blocks = [zero_block] + [block(a, b) for a in range(3)] + [zero_block]
            for a in range(4):
                at = (3 * a + b) * CH
                ref[at : at + CH, :] = jnp.concatenate([blocks[a + 1], blocks[a]], axis=1)

    place_weights(fwd_w, lambda a, b: pair_ref[(3 * a + b) * CH : (3 * a + b + 1) * CH, :])

    zero_row = jnp.zeros((160, CH), BF16)
    hid[0] = zero_row
    hid[33] = zero_row
    cgrad[0] = zero_row
    cgrad[33] = zero_row

    wait_recv(0, stat_in)
    early = jnp.sum(stat_in[...], axis=0)
    wait_recv(1, late_in)
    late = jnp.sum(late_in[...], axis=0)
    mean = jnp.concatenate([early[0:4], late[0:2]], axis=0) / BINS
    var = jnp.concatenate([early[4:8], late[2:4]], axis=0) / BINS - mean * mean
    scale = lax.rsqrt(var + 1e-05)
    normed = jnp.concatenate(
        [
            ((pooled2[q] - mean[q : q + 1]) * scale[q : q + 1]).astype(BF16)
            for q in range(TILES)
        ],
        axis=1,
    )
    emb = jnp.dot(normed, proj[...], preferred_element_type=F32)
    rows_emb = emb[:, 0:CH]
    cols_emb = emb[:, CH : 2 * CH]
    zero_six = jnp.zeros((6, CH), F32)
    for h in range(2):
        block = [cols_emb[4 * h : 4 * h + 4], cols_emb[8 + 4 * h : 12 + 4 * h]]
        for r in range(8):
            pair = [rows_emb[r : r + 1], rows_emb[r + 8 : r + 9]]
            emb_out[2 * r + h] = jnp.concatenate(block + pair + [zero_six], 0).astype(BF16)
    send_all(2, lambda peer: emb_out.at[peer], emb_in)
    emb_in[pl.ds(me, 1)] = emb_out[pl.ds(me, 1)]

    place_weights(
        bwd_w, lambda a, b: pair_ref[(8 - 3 * a - b) * CH : (9 - 3 * a - b) * CH, :].T
    )
    tgt_rows[...] = jnp.zeros_like(tgt_rows)
    for d in range(N_SEQ):
        tgt_rows[2 * d : 2 * d + 2, :] = late_in[d, 4:6, :]
    tgt_t[...] = tgt_rows[...].T

    def chain_order(load):
        pieces = []
        for q in range(8):
            for s in range(4):
                pieces.append(load(q + 8 * s))
        return jnp.concatenate(pieces, axis=0)

    target = chain_order(lambda m: tgt_t[pl.ds(8 * m + 4 * half, 4), :])
    target = (target - 7.5) * 0.25

    wait_recv(2, emb_in)

    embs = [emb_in[d].astype(F32) for d in range(N_SEQ)]
    for d in range(N_SEQ):
        rows_scr[2 * d : 2 * d + 2, :] = embs[d][8:10]
    cols = chain_order(lambda m: embs[m // 2][4 * (m % 2) : 4 * (m % 2) + 4])
    zero_four = jnp.zeros((4, CH), F32)

    def put_row(ref, index, values):
        ref[index, 16:144, :] = values.astype(BF16)
        ref[index, 0:16, :] = jnp.concatenate([zero_four, values[112:124]], axis=0).astype(BF16)
        ref[index, 144:160, :] = jnp.concatenate([values[4:16], zero_four], axis=0).astype(BF16)

    def hidden_body(u, carry):
        summed = cols + rows_scr[pl.ds(u, 1), :]
        value, slope = gelu_and_slope(summed)
        slope_scr[u] = slope
        put_row(hid, u + 1, value)
        return carry

    lax.fori_loop(0, 32, hidden_body, 0, unroll=4)

    out_scale = out_w_ref[...].astype(F32)
    small_scale = out_scale * (1.0 / math.sqrt(BINS))
    chain_lane = lax.broadcasted_iota(jnp.int32, (CH, CH), 1)

    def conv_pairs(ref, weights, v, count):
        blocks = []
        for c in range(count):
            row = 2 * (v * count + c)
            blocks.append(
                jnp.concatenate(
                    [
                        ref[row + a, 16 * b : 16 * b + 128, :]
                        for a in range(4)
                        for b in range(3)
                    ],
                    axis=1,
                )
            )
        return jnp.dot(jnp.concatenate(blocks, axis=0), weights, preferred_element_type=F32)

    PAIRS = 8

    def forward_body(v, diff):
        conv = conv_pairs(hid, fwd_w[...], v, PAIRS)
        for c in range(PAIRS):
            for e in range(2):
                u = 2 * (v * PAIRS + c) + e
                out = conv[128 * c : 128 * c + 128, CH * e : CH * e + CH]
                value, slope = gelu_and_slope(out)
                summed = (hid[u + 1, 16:144, :].astype(F32) + value) * out_scale
                summed = summed - jnp.where(chain_lane == u, target, 0.0)
                error = jnp.sum(summed, axis=1, keepdims=True)
                direct = error * small_scale
                direct_scr[u] = direct
                put_row(cgrad, u + 1, direct * slope)
                diff = jnp.where(chain_lane == u, error, diff)
        return diff

    errors = lax.fori_loop(0, 16 // PAIRS, forward_body, jnp.zeros((CH, CH), F32))
    predicted = errors + target

    def backward_body(v, colsum):
        conv = conv_pairs(cgrad, bwd_w[...], v, PAIRS)
        for c in range(PAIRS):
            for e in range(2):
                u = 2 * (v * PAIRS + c) + e
                out = conv[128 * c : 128 * c + 128, CH * e : CH * e + CH]
                grad = (direct_scr[u] + out) * slope_scr[u]
                rowsum[pl.ds(u, 1), :] = jnp.sum(grad, axis=0, keepdims=True)
                colsum = colsum + grad
        return colsum

    colsum = lax.fori_loop(0, 16 // PAIRS, backward_body, jnp.zeros((CH, CH), F32))

    pred_t[...] = jnp.zeros_like(pred_t)
    for q in range(8):
        for s in range(4):
            at = 16 * q + 4 * s
            pred_t[pl.ds(8 * (q + 8 * s) + 4 * half, 4), :] = predicted[at : at + 4]
    home = pred_t[...].T
    for d in range(N_SEQ):
        for e in range(2):
            m = 2 * d + e
            at = 16 * (m % 8) + 4 * (m // 8)
            part_out[d, 4 * e : 4 * e + 4, :] = colsum[at : at + 4]
            part_out[d, 10 + e : 11 + e, :] = home[m : m + 1, 0:CH]
            part_out[d, 12 + e : 13 + e, :] = home[m : m + 1, CH : 2 * CH]
        part_out[d, 8:10, :] = rowsum[2 * d : 2 * d + 2, :]
        part_out[d, 14:16, :] = jnp.zeros((2, CH), F32)
    send_all(3, lambda peer: part_out.at[peer], part_in)
    part_in[pl.ds(me, 1)] = part_out[pl.ds(me, 1)]

    wait_recv(3, part_in)
    for r in range(8):
        both = part_in[2 * r, 10:14, :] + part_in[2 * r + 1, 10:14, :]
        for e in range(2):
            pred_ref[r + 8 * e : r + 8 * e + 1, 0:CH] = both[e : e + 1]
            pred_ref[r + 8 * e : r + 8 * e + 1, CH : 2 * CH] = both[2 + e : 3 + e]
    col_halves = []
    for h in range(2):
        total = part_in[h, 0:8, :]
        for r in range(1, 8):
            total = total + part_in[2 * r + h, 0:8, :]
        col_halves.append(total)
    col_grad = jnp.concatenate(
        [
            col_halves[0][0:4],
            col_halves[1][0:4],
            col_halves[0][4:8],
            col_halves[1][4:8],
        ],
        axis=0,
    )
    row_pairs = [part_in[2 * r, 8:10, :] + part_in[2 * r + 1, 8:10, :] for r in range(8)]
    row_grad = jnp.concatenate(
        [pair[0:1] for pair in row_pairs] + [pair[1:2] for pair in row_pairs], axis=0
    )
    grads = jnp.concatenate([row_grad, col_grad], axis=1)
    high = grads.astype(BF16)
    rest = grads - high.astype(F32)
    middle = rest.astype(BF16)
    low = (rest - middle.astype(F32)).astype(BF16)
    stacked = jnp.concatenate([high, middle, low], axis=0)
    wide = lax.dot_general(
        stacked,
        proj[...],
        (((1,), (1,)), ((), ())),
        preferred_element_type=F32,
    )
    grad_ref[...] = (wide[32:48] + wide[16:32]) + wide[0:16]

    wait_send(0, stat_in)
    wait_send(1, late_in)
    wait_send(2, emb_in)
    wait_send(3, part_in)


def deliver(pred_in, grad_in, pred_out, grad_out):
    pred_out[...] = pred_in[...]
    grad_out[...] = grad_in[...]


def per_device(
    bases, stem_weight, conv_weight, row_proj, col_proj, pair_weight, out_weight, targets
):
    vmem = pl.BlockSpec(memory_space=pltpu.VMEM)
    hbm = pl.BlockSpec(memory_space=pl.ANY)
    shapes = (
        jax.ShapeDtypeStruct((LOCAL, BINS), F32),
        jax.ShapeDtypeStruct((LOCAL, TRUNK_CH), F32),
    )
    results = pl.pallas_call(
        fused,
        out_shape=shapes,
        in_specs=[hbm] * 8,
        out_specs=(vmem, vmem),
        scratch_shapes=[
            pltpu.VMEM((ROWS, POOL), jnp.int32),
            pltpu.VMEM((20, STEM_CH), BF16),
            pltpu.VMEM((1, CH), BF16),
            pltpu.VMEM((LOCAL, BINS), jnp.int32),
            pltpu.VMEM((2, 8, POOL), jnp.int32),
            pltpu.VMEM((ROWS + 16, POOL), jnp.int32),
            pltpu.VMEM((ROWS, POOL), jnp.int32),
            pltpu.VMEM((264, POOL), jnp.int32),
            pltpu.VMEM((32, STEM_CH), F32),
            pltpu.VMEM((2, GROUP * POOL, 32), BF16),
            pltpu.VMEM((2, GROUP, STEM_CH), F32),
            pltpu.VMEM((12 * GROUP, STEM_CH), F32),
            pltpu.VMEM((20 * 16, STEM_CH), BF16),
            pltpu.VMEM((TILES, 5 * STEM_CH, 256), BF16),
            pltpu.VMEM((TILES, LOCAL, 256), F32),
            pltpu.VMEM((TRUNK_CH, 2 * CH), BF16),
            pltpu.VMEM((9 * CH, CH), BF16),
            pltpu.VMEM((16, 256), F32),
            pltpu.VMEM((8, 256), F32),
            pltpu.VMEM((N_SEQ, 8, 256), F32),
            pltpu.VMEM((8, 8, 256), F32),
            pltpu.VMEM((N_SEQ, 8, 256), F32),
            pltpu.VMEM((N_SEQ, 16, CH), BF16),
            pltpu.VMEM((N_SEQ, 16, CH), BF16),
            pltpu.VMEM((CH, BINS), F32),
            pltpu.VMEM((BINS, CH), F32),
            pltpu.VMEM((12 * CH, 2 * CH), BF16),
            pltpu.VMEM((12 * CH, 2 * CH), BF16),
            pltpu.VMEM((32, CH), F32),
            pltpu.VMEM((34, 160, CH), BF16),
            pltpu.VMEM((32, CH, CH), F32),
            pltpu.VMEM((32, CH, CH), F32),
            pltpu.VMEM((34, 160, CH), BF16),
            pltpu.VMEM((BINS, CH), F32),
            pltpu.VMEM((32, CH), F32),
            pltpu.VMEM((N_SEQ, 16, CH), F32),
            pltpu.VMEM((N_SEQ, 16, CH), F32),
            pltpu.SemaphoreType.DMA((4,)),
            pltpu.SemaphoreType.DMA((TILES,)),
            pltpu.SemaphoreType.DMA((3,)),
            pltpu.SemaphoreType.DMA((2,)),
            pltpu.SemaphoreType.DMA((2,)),
            pltpu.SemaphoreType.DMA((4,)),
            pltpu.SemaphoreType.DMA((4,)),
        ],
        compiler_params=pltpu.CompilerParams(
            collective_id=0, has_side_effects=True, vmem_limit_bytes=56 << 20
        ),
    )(
        bases.reshape(ROWS, POOL),
        stem_weight,
        conv_weight.reshape(5 * STEM_CH, TRUNK_CH),
        row_proj,
        col_proj,
        pair_weight.reshape(9 * CH, CH),
        out_weight.reshape(1, CH),
        targets,
    )
    return pl.pallas_call(
        deliver, out_shape=shapes, in_specs=[vmem, vmem], out_specs=(vmem, vmem)
    )(*results)


def solution(mesh):
    in_specs = (P(("dp", "seq")), P(), P(), P(), P(), P(), P(), P(("dp", "seq"), None))
    out_specs = (P(("dp", "seq"), None), P(("dp", "seq"), None))
    return jax.shard_map(
        per_device, mesh=mesh, in_specs=in_specs, out_specs=out_specs, check_vma=False
    )
```

```python
import functools
import math

import jax
import jax.numpy as jnp
from jax import lax
from jax.experimental import pallas as pl
from jax.experimental.pallas import tpu as pltpu
from jax.sharding import PartitionSpec as P

MESH = pl.DeviceIdType.MESH
FAR_FIRST = sorted(
    [(z, x, c) for z in range(2) for x in range(4) for c in range(2) if (z, x, c) != (0, 0, 0)],
    key=lambda d: -(d[0] + min(d[1], 4 - d[1]) + 0.1 * d[2]),
)
F32 = jnp.float32
BF16 = jnp.bfloat16

N_SEQ = 16
STEM_CH = 768
TRUNK_CH = 1536
CH = 128
POOL = 128
ROWS = 256
BINS = 256
LOCAL = 16
GROUP = 24
TILES = TRUNK_CH // 256
C0 = math.sqrt(2.0 / math.pi)


def gelu(x):
    half = 0.5 * x
    return half + half * jnp.tanh(x * (C0 + (C0 * 0.044715) * (x * x)))


def gelu_and_slope(x):
    square = x * x
    a = 0.5 + 0.5 * jnp.tanh(x * (C0 + (C0 * 0.044715) * square))
    value = x * a
    slope = a + value * (1.0 - a) * (2.0 * C0 + (6.0 * C0 * 0.044715) * square)
    return value, slope


def fused(
    bases_hbm,
    stem_hbm,
    conv_ref,
    row_proj_ref,
    col_proj_ref,
    pair_hbm,
    out_w_hbm,
    targets_hbm,
    pred_ref,
    grad_ref,
    bases_ref,
    stem_ref,
    out_w_ref,
    targets_ref,
    halo,
    ext,
    codes_in_order,
    codes,
    stem_w,
    onehot,
    extremes,
    pooled1,
    taps,
    conv_w,
    pooled2,
    proj,
    pair_ref,
    stat_all,
    stat_out,
    stat_in,
    late_out,
    late_in,
    emb_out,
    emb_in,
    tgt_rows,
    tgt_t,
    fwd_w,
    bwd_w,
    rows_scr,
    hid,
    slope_scr,
    direct_scr,
    cgrad,
    pred_t,
    rowsum,
    part_out,
    part_in,
    input_sems,
    conv_sems,
    weight_sems,
    halo_send,
    halo_recv,
    send_sems,
    recv_sems,
):
    me = lax.axis_index("seq")
    rho = me // 2
    half = me % 2
    z, x, core = me // 8, lax.rem(me // 2, 4), half
    first = me == 0
    last = me == N_SEQ - 1

    input_copies = [
        pltpu.make_async_copy(bases_hbm, bases_ref, input_sems.at[0]),
        pltpu.make_async_copy(stem_hbm, stem_ref, input_sems.at[1]),
        pltpu.make_async_copy(out_w_hbm, out_w_ref, input_sems.at[2]),
        pltpu.make_async_copy(targets_hbm, targets_ref, input_sems.at[3]),
    ]
    for copy in input_copies:
        copy.start()
    conv_copies = [
        pltpu.make_async_copy(
            conv_ref.at[:, pl.ds(256 * q, 256)], conv_w.at[q], conv_sems.at[q]
        )
        for q in range(TILES)
    ]
    weight_copies = [
        pltpu.make_async_copy(row_proj_ref, proj.at[:, pl.ds(0, CH)], weight_sems.at[0]),
        pltpu.make_async_copy(col_proj_ref, proj.at[:, pl.ds(CH, CH)], weight_sems.at[1]),
        pltpu.make_async_copy(pair_hbm, pair_ref, weight_sems.at[2]),
    ]

    barrier = pltpu.get_barrier_semaphore()

    def greet(k, carry):
        peer = lax.rem(me + k, N_SEQ)
        pl.semaphore_signal(barrier, inc=1, device_id={"seq": peer}, device_id_type=MESH)
        return carry

    lax.fori_loop(1, N_SEQ, greet, 0)

    ext[...] = jnp.zeros_like(ext)
    for copy in input_copies:
        copy.wait()
    ext[8 : 8 + ROWS, :] = bases_ref[...] + 1
    stem_w[...] = jnp.zeros_like(stem_w)
    stem_w[0:20, :] = stem_ref[...].astype(F32)

    def send_all(index, source_of, landing):
        for dz, dx, dc in FAR_FIRST:
            peer = 8 * lax.rem(z + dz, 2) + 2 * lax.rem(x + dx, 4) + lax.rem(core + dc, 2)
            pltpu.make_async_remote_copy(
                src_ref=source_of(peer),
                dst_ref=landing.at[me],
                send_sem=send_sems.at[index],
                recv_sem=recv_sems.at[index],
                device_id={"seq": peer},
                device_id_type=MESH,
            ).start()

    def wait_recv(index, landing):
        blocks = landing.at[pl.ds(0, N_SEQ - 1)]
        pltpu.make_async_copy(blocks, blocks, recv_sems.at[index]).wait()

    def wait_send(index, landing):
        blocks = landing.at[pl.ds(0, N_SEQ - 1)]
        pltpu.make_async_copy(blocks, blocks, send_sems.at[index]).wait()

    lane = lax.broadcasted_iota(jnp.int32, (1, POOL), 1)

    def code_rows(start, count):
        total = ext[start : start + count, :] << 6
        here = ext[start : start + count, :]
        above = ext[start - 1 : start - 1 + count, :]
        below = ext[start + 1 : start + 1 + count, :]
        for shift in (1, 2):
            before = jnp.where(
                lane >= shift, pltpu.roll(here, shift, 1), pltpu.roll(above, shift, 1)
            )
            after = jnp.where(
                lane < POOL - shift,
                pltpu.roll(here, POOL - shift, 1),
                pltpu.roll(below, POOL - shift, 1),
            )
            total = total + (before << (3 * (2 - shift))) + (after << (3 * (2 + shift)))
        return total

    codes_in_order[0:ROWS, :] = code_rows(8, ROWS)
    for q in range(1, 15):
        codes[16 * (q - 1) : 16 * q, :] = codes_in_order[pl.ds(q, 16, stride=16), :]

    sub = lax.broadcasted_iota(jnp.int32, (8, POOL), 0)
    base_code = (sub & 3) + 1
    tap_shift = (sub >> 2) * 3
    zero_rows = jnp.zeros((8, POOL), F32)

    def onehot_rows(start, r):
        code = jnp.broadcast_to(codes[pl.ds(start + r, 1), :], (8, POOL))
        pairs = [
            jnp.where(((code >> (tap_shift + 6 * k)) & 7) == base_code, 1.0, 0.0).astype(F32)
            for k in range(3)
        ]
        return jnp.concatenate(pairs + [zero_rows], axis=0).astype(BF16).T

    def pooled_rows():
        values = jnp.maximum(gelu(extremes[0]), gelu(extremes[1]))
        return values.astype(BF16).astype(F32)

    up = pltpu.make_async_remote_copy(
        src_ref=bases_ref.at[pl.ds(ROWS - 8, 8)],
        dst_ref=halo.at[0],
        send_sem=halo_send.at[0],
        recv_sem=halo_recv.at[0],
        device_id={"seq": lax.rem(me + 1, N_SEQ)},
        device_id_type=MESH,
    )
    down = pltpu.make_async_remote_copy(
        src_ref=bases_ref.at[pl.ds(0, 8)],
        dst_ref=halo.at[1],
        send_sem=halo_send.at[1],
        recv_sem=halo_recv.at[1],
        device_id={"seq": lax.rem(me + N_SEQ - 1, N_SEQ)},
        device_id_type=MESH,
    )

    def first_onehot(r, carry):
        onehot[0, pl.ds(pl.multiple_of(POOL * r, POOL), POOL), :] = onehot_rows(0, r)
        return carry

    lax.fori_loop(0, GROUP, first_onehot, 0, unroll=12)
    extremes[...] = jnp.zeros_like(extremes)

    def stem_body(g, carry):
        @pl.when(g == 2)
        def _():
            pl.semaphore_wait(barrier, N_SEQ - 1)
            up.start()
            down.start()
            for copy in conv_copies + weight_copies:
                copy.start()

        @pl.when(g == 8)
        def _():
            up.wait()
            down.wait()
            ext[0:8, :] = jnp.where(first, 0, halo[0] + 1)
            ext[8 + ROWS : 16 + ROWS, :] = jnp.where(last, 0, halo[1] + 1)
            begin = code_rows(6, 3)
            end = code_rows(7 + ROWS, 3)
            codes_in_order[0:1, :] = begin[2:3]
            codes_in_order[ROWS - 1 : ROWS, :] = end[0:1]
            codes[224:240, :] = codes_in_order[pl.ds(0, 16, stride=16), :]
            codes[240:256, :] = codes_in_order[pl.ds(15, 16, stride=16), :]
            codes[256:258, :] = begin[0:2]
            codes[258:260, :] = end[1:3]
            codes[260:264, :] = jnp.zeros((4, POOL), jnp.int32)

        @pl.when(g == 10)
        def _():
            for copy in conv_copies:
                copy.wait()

        slot = lax.rem(g, 2)
        pooled1[pl.ds(pl.multiple_of(g * GROUP, 8), GROUP), :] = pooled_rows()
        for n in range(STEM_CH // 256):
            stem = jnp.dot(
                onehot[slot],
                stem_w[:, 256 * n : 256 * n + 256].astype(BF16),
                preferred_element_type=F32,
            ).reshape(GROUP, POOL, 256)
            extremes[0, :, 256 * n : 256 * n + 256] = jnp.max(stem, axis=1)
            extremes[1, :, 256 * n : 256 * n + 256] = jnp.min(stem, axis=1)
        start = pl.multiple_of(jnp.minimum(g + 1, 10) * GROUP, 8)
        for r in range(GROUP):
            onehot[1 - slot, POOL * r : POOL * r + POOL, :] = onehot_rows(start, r)
        return carry

    lax.fori_loop(0, 11, stem_body, 0)
    pooled1[11 * GROUP : 12 * GROUP, :] = pooled_rows()

    for r in range(8):
        for e in range(2):
            late_out[r, 4 + e : 5 + e, :] = targets_ref[r + 8 * e : r + 8 * e + 1, :].astype(F32)
        late_out[r, 6:8, :] = jnp.zeros((2, 256), F32)

    def stem_tile(q):
        at = GROUP + (16 * (q - 1) if 1 <= q <= 14 else 224 + (q // 15) * 16)
        return pooled1[at : at + 16, :]

    outer = pooled1[GROUP + 256 : GROUP + 264, :]
    before = jnp.where(first, 0.0, outer[0:2])
    after = jnp.where(last, 0.0, outer[2:4])
    for q in range(16):
        taps[16 * (q + 2) : 16 * (q + 3), :] = stem_tile(q).astype(BF16)
    for e in range(2):
        taps[16 * e : 16 * e + 16, :] = jnp.concatenate(
            [before[e : e + 1], stem_tile(14 + e)[0:15]], axis=0
        ).astype(BF16)
        taps[16 * (18 + e) : 16 * (19 + e), :] = jnp.concatenate(
            [stem_tile(e)[1:16], after[e : e + 1]], axis=0
        ).astype(BF16)

    def trunk_tile(q):
        windows = [taps[16 * k : 16 * k + ROWS, :] for k in range(5)]
        trunk = jnp.dot(
            jnp.concatenate(windows, axis=1), conv_w[q], preferred_element_type=F32
        ).reshape(16, LOCAL, 256)
        block = jnp.maximum(gelu(jnp.max(trunk, axis=0)), gelu(jnp.min(trunk, axis=0)))
        pooled2[q] = block
        total = jnp.sum(block, axis=0, keepdims=True)
        return total, jnp.sum(block * block, axis=0, keepdims=True)

    for q in range(TILES):
        total, square = trunk_tile(q)
        stat_all[q : q + 1, :] = total
        stat_all[8 + q : 9 + q, :] = square
        if q == 3:
            stat_out[0:4, :] = stat_all[0:4, :]
            stat_out[4:8, :] = stat_all[8:12, :]
            send_all(0, lambda peer: stat_out, stat_in)
    stat_in[pl.ds(me, 1)] = stat_out[...][None]
    for r in range(8):
        late_out[r, 0:2, :] = stat_all[4:6, :]
        late_out[r, 2:4, :] = stat_all[12:14, :]
    send_all(1, lambda peer: late_out.at[peer // 2], late_in)
    late_in[pl.ds(me, 1)] = late_out[pl.ds(rho, 1)]

    for copy in weight_copies:
        copy.wait()
    zero_block = jnp.zeros((CH, CH), BF16)

    def place_weights(ref, block):
        for b in range(3):
            blocks = [zero_block] + [block(a, b) for a in range(3)] + [zero_block]
            for a in range(4):
                at = (3 * a + b) * CH
                ref[at : at + CH, :] = jnp.concatenate([blocks[a + 1], blocks[a]], axis=1)

    place_weights(fwd_w, lambda a, b: pair_ref[(3 * a + b) * CH : (3 * a + b + 1) * CH, :])

    zero_row = jnp.zeros((160, CH), BF16)
    hid[0] = zero_row
    hid[33] = zero_row
    cgrad[0] = zero_row
    cgrad[33] = zero_row

    wait_recv(0, stat_in)
    early = jnp.sum(stat_in[...], axis=0)
    wait_recv(1, late_in)
    late = jnp.sum(late_in[...], axis=0)
    mean = jnp.concatenate([early[0:4], late[0:2]], axis=0) / BINS
    var = jnp.concatenate([early[4:8], late[2:4]], axis=0) / BINS - mean * mean
    scale = lax.rsqrt(var + 1e-05)
    normed = jnp.concatenate(
        [
            ((pooled2[q] - mean[q : q + 1]) * scale[q : q + 1]).astype(BF16)
            for q in range(TILES)
        ],
        axis=1,
    )
    emb = jnp.dot(normed, proj[...], preferred_element_type=F32)
    rows_emb = emb[:, 0:CH]
    cols_emb = emb[:, CH : 2 * CH]
    zero_six = jnp.zeros((6, CH), F32)
    for h in range(2):
        block = [cols_emb[4 * h : 4 * h + 4], cols_emb[8 + 4 * h : 12 + 4 * h]]
        for r in range(8):
            pair = [rows_emb[r : r + 1], rows_emb[r + 8 : r + 9]]
            emb_out[2 * r + h] = jnp.concatenate(block + pair + [zero_six], 0).astype(BF16)
    send_all(2, lambda peer: emb_out.at[peer], emb_in)
    emb_in[pl.ds(me, 1)] = emb_out[pl.ds(me, 1)]

    place_weights(
        bwd_w, lambda a, b: pair_ref[(8 - 3 * a - b) * CH : (9 - 3 * a - b) * CH, :].T
    )
    tgt_rows[...] = jnp.zeros_like(tgt_rows)
    for d in range(N_SEQ):
        tgt_rows[2 * d : 2 * d + 2, :] = late_in[d, 4:6, :]
    tgt_t[...] = tgt_rows[...].T

    def chain_order(load):
        pieces = []
        for q in range(8):
            for s in range(4):
                pieces.append(load(q + 8 * s))
        return jnp.concatenate(pieces, axis=0)

    target = chain_order(lambda m: tgt_t[pl.ds(8 * m + 4 * half, 4), :])
    target = (target - 7.5) * 0.25

    wait_recv(2, emb_in)

    embs = [emb_in[d].astype(F32) for d in range(N_SEQ)]
    for d in range(N_SEQ):
        rows_scr[2 * d : 2 * d + 2, :] = embs[d][8:10]
    cols = chain_order(lambda m: embs[m // 2][4 * (m % 2) : 4 * (m % 2) + 4])
    zero_four = jnp.zeros((4, CH), F32)

    def put_row(ref, index, values):
        ref[index, 16:144, :] = values.astype(BF16)
        ref[index, 0:16, :] = jnp.concatenate([zero_four, values[112:124]], axis=0).astype(BF16)
        ref[index, 144:160, :] = jnp.concatenate([values[4:16], zero_four], axis=0).astype(BF16)

    def hidden_body(u, carry):
        summed = cols + rows_scr[pl.ds(u, 1), :]
        value, slope = gelu_and_slope(summed)
        slope_scr[u] = slope
        put_row(hid, u + 1, value)
        return carry

    lax.fori_loop(0, 32, hidden_body, 0, unroll=4)

    out_scale = out_w_ref[...].astype(F32)
    small_scale = out_scale * (1.0 / math.sqrt(BINS))
    chain_lane = lax.broadcasted_iota(jnp.int32, (CH, CH), 1)

    def conv_pairs(ref, weights, v, count):
        blocks = []
        for c in range(count):
            row = 2 * (v * count + c)
            blocks.append(
                jnp.concatenate(
                    [
                        ref[row + a, 16 * b : 16 * b + 128, :]
                        for a in range(4)
                        for b in range(3)
                    ],
                    axis=1,
                )
            )
        return jnp.dot(jnp.concatenate(blocks, axis=0), weights, preferred_element_type=F32)

    PAIRS = 8

    def forward_body(v, diff):
        conv = conv_pairs(hid, fwd_w[...], v, PAIRS)
        for c in range(PAIRS):
            for e in range(2):
                u = 2 * (v * PAIRS + c) + e
                out = conv[128 * c : 128 * c + 128, CH * e : CH * e + CH]
                value, slope = gelu_and_slope(out)
                summed = (hid[u + 1, 16:144, :].astype(F32) + value) * out_scale
                summed = summed - jnp.where(chain_lane == u, target, 0.0)
                error = jnp.sum(summed, axis=1, keepdims=True)
                direct = error * small_scale
                direct_scr[u] = direct
                put_row(cgrad, u + 1, direct * slope)
                diff = jnp.where(chain_lane == u, error, diff)
        return diff

    errors = lax.fori_loop(0, 16 // PAIRS, forward_body, jnp.zeros((CH, CH), F32))
    predicted = errors + target

    def backward_body(v, colsum):
        conv = conv_pairs(cgrad, bwd_w[...], v, PAIRS)
        for c in range(PAIRS):
            for e in range(2):
                u = 2 * (v * PAIRS + c) + e
                out = conv[128 * c : 128 * c + 128, CH * e : CH * e + CH]
                grad = (direct_scr[u] + out) * slope_scr[u]
                rowsum[pl.ds(u, 1), :] = jnp.sum(grad, axis=0, keepdims=True)
                colsum = colsum + grad
        return colsum

    colsum = lax.fori_loop(0, 16 // PAIRS, backward_body, jnp.zeros((CH, CH), F32))

    pred_t[...] = jnp.zeros_like(pred_t)
    for q in range(8):
        for s in range(4):
            at = 16 * q + 4 * s
            pred_t[pl.ds(8 * (q + 8 * s) + 4 * half, 4), :] = predicted[at : at + 4]
    home = pred_t[...].T
    for d in range(N_SEQ):
        for e in range(2):
            m = 2 * d + e
            at = 16 * (m % 8) + 4 * (m // 8)
            part_out[d, 4 * e : 4 * e + 4, :] = colsum[at : at + 4]
            part_out[d, 10 + e : 11 + e, :] = home[m : m + 1, 0:CH]
            part_out[d, 12 + e : 13 + e, :] = home[m : m + 1, CH : 2 * CH]
        part_out[d, 8:10, :] = rowsum[2 * d : 2 * d + 2, :]
        part_out[d, 14:16, :] = jnp.zeros((2, CH), F32)
    send_all(3, lambda peer: part_out.at[peer], part_in)
    part_in[pl.ds(me, 1)] = part_out[pl.ds(me, 1)]

    wait_recv(3, part_in)
    for r in range(8):
        both = part_in[2 * r, 10:14, :] + part_in[2 * r + 1, 10:14, :]
        for e in range(2):
            pred_ref[r + 8 * e : r + 8 * e + 1, 0:CH] = both[e : e + 1]
            pred_ref[r + 8 * e : r + 8 * e + 1, CH : 2 * CH] = both[2 + e : 3 + e]
    col_halves = []
    for h in range(2):
        total = part_in[h, 0:8, :]
        for r in range(1, 8):
            total = total + part_in[2 * r + h, 0:8, :]
        col_halves.append(total)
    col_grad = jnp.concatenate(
        [
            col_halves[0][0:4],
            col_halves[1][0:4],
            col_halves[0][4:8],
            col_halves[1][4:8],
        ],
        axis=0,
    )
    row_pairs = [part_in[2 * r, 8:10, :] + part_in[2 * r + 1, 8:10, :] for r in range(8)]
    row_grad = jnp.concatenate(
        [pair[0:1] for pair in row_pairs] + [pair[1:2] for pair in row_pairs], axis=0
    )
    grads = jnp.concatenate([row_grad, col_grad], axis=1)
    high = grads.astype(BF16)
    rest = grads - high.astype(F32)
    middle = rest.astype(BF16)
    low = (rest - middle.astype(F32)).astype(BF16)
    stacked = jnp.concatenate([high, middle, low], axis=0)
    wide = lax.dot_general(
        stacked,
        proj[...],
        (((1,), (1,)), ((), ())),
        preferred_element_type=F32,
    )
    grad_ref[...] = (wide[32:48] + wide[16:32]) + wide[0:16]

    wait_send(0, stat_in)
    wait_send(1, late_in)
    wait_send(2, emb_in)
    wait_send(3, part_in)


def deliver(pred_in, grad_in, pred_out, grad_out):
    pred_out[...] = pred_in[...]
    grad_out[...] = grad_in[...]


def per_device(
    bases, stem_weight, conv_weight, row_proj, col_proj, pair_weight, out_weight, targets
):
    vmem = pl.BlockSpec(memory_space=pltpu.VMEM)
    hbm = pl.BlockSpec(memory_space=pl.ANY)
    shapes = (
        jax.ShapeDtypeStruct((LOCAL, BINS), F32),
        jax.ShapeDtypeStruct((LOCAL, TRUNK_CH), F32),
    )
    results = pl.pallas_call(
        fused,
        out_shape=shapes,
        in_specs=[hbm] * 8,
        out_specs=(vmem, vmem),
        scratch_shapes=[
            pltpu.VMEM((ROWS, POOL), jnp.int32),
            pltpu.VMEM((20, STEM_CH), BF16),
            pltpu.VMEM((1, CH), BF16),
            pltpu.VMEM((LOCAL, BINS), jnp.int32),
            pltpu.VMEM((2, 8, POOL), jnp.int32),
            pltpu.VMEM((ROWS + 16, POOL), jnp.int32),
            pltpu.VMEM((ROWS + 16, POOL), jnp.int32),
            pltpu.VMEM((264, POOL), jnp.int32),
            pltpu.VMEM((32, STEM_CH), F32),
            pltpu.VMEM((2, GROUP * POOL, 32), BF16),
            pltpu.VMEM((2, GROUP, STEM_CH), F32),
            pltpu.VMEM((12 * GROUP, STEM_CH), F32),
            pltpu.VMEM((20 * 16, STEM_CH), BF16),
            pltpu.VMEM((TILES, 5 * STEM_CH, 256), BF16),
            pltpu.VMEM((TILES, LOCAL, 256), F32),
            pltpu.VMEM((TRUNK_CH, 2 * CH), BF16),
            pltpu.VMEM((9 * CH, CH), BF16),
            pltpu.VMEM((16, 256), F32),
            pltpu.VMEM((8, 256), F32),
            pltpu.VMEM((N_SEQ, 8, 256), F32),
            pltpu.VMEM((8, 8, 256), F32),
            pltpu.VMEM((N_SEQ, 8, 256), F32),
            pltpu.VMEM((N_SEQ, 16, CH), BF16),
            pltpu.VMEM((N_SEQ, 16, CH), BF16),
            pltpu.VMEM((CH, BINS), F32),
            pltpu.VMEM((BINS, CH), F32),
            pltpu.VMEM((12 * CH, 2 * CH), BF16),
            pltpu.VMEM((12 * CH, 2 * CH), BF16),
            pltpu.VMEM((32, CH), F32),
            pltpu.VMEM((34, 160, CH), BF16),
            pltpu.VMEM((32, CH, CH), F32),
            pltpu.VMEM((32, CH, CH), F32),
            pltpu.VMEM((34, 160, CH), BF16),
            pltpu.VMEM((BINS, CH), F32),
            pltpu.VMEM((32, CH), F32),
            pltpu.VMEM((N_SEQ, 16, CH), F32),
            pltpu.VMEM((N_SEQ, 16, CH), F32),
            pltpu.SemaphoreType.DMA((4,)),
            pltpu.SemaphoreType.DMA((TILES,)),
            pltpu.SemaphoreType.DMA((3,)),
            pltpu.SemaphoreType.DMA((2,)),
            pltpu.SemaphoreType.DMA((2,)),
            pltpu.SemaphoreType.DMA((4,)),
            pltpu.SemaphoreType.DMA((4,)),
        ],
        compiler_params=pltpu.CompilerParams(
            collective_id=0, has_side_effects=True, vmem_limit_bytes=56 << 20
        ),
    )(
        bases.reshape(ROWS, POOL),
        stem_weight,
        conv_weight.reshape(5 * STEM_CH, TRUNK_CH),
        row_proj,
        col_proj,
        pair_weight.reshape(9 * CH, CH),
        out_weight.reshape(1, CH),
        targets,
    )
    return pl.pallas_call(
        deliver, out_shape=shapes, in_specs=[vmem, vmem], out_specs=(vmem, vmem)
    )(*results)


def solution(mesh):
    in_specs = (P(("dp", "seq")), P(), P(), P(), P(), P(), P(), P(("dp", "seq"), None))
    out_specs = (P(("dp", "seq"), None), P(("dp", "seq"), None))
    return jax.shard_map(
        per_device, mesh=mesh, in_specs=in_specs, out_specs=out_specs, check_vma=False
    )
```
